32 devices in a mesh: gx: 4 (over y, core), gy: 2 (over x), gz: 4 (over z).
Axes of the slice: x: 2, y: 2, z: 4, core: 2. Of those that a mesh axis runs over, the one named last changes fastest.
Arguments:
- populations: float32 [19, 16, 16, 512], P(None, 'gz', 'gy', 'gx'), as said below
- porosity: float32 [16, 16, 512], P('gz', 'gy', 'gx'), may hold values from 0 to 1
- node_type: int32 [16, 16, 512], P('gz', 'gy', 'gx'), may hold values from 0 to 3, as said below
- step_index: int32 [1], replicated, may hold values from 0 to 4095
- adjoint_end: float32 [19, 16, 16, 512], P(None, 'gz', 'gy', 'gx'), may hold values from -6 to 6
Outputs:
- adjoint_start: float32 [19, 16, 16, 512], P(None, 'gz', 'gy', 'gx')
- sensitivity: float32 [16, 16, 512], P('gz', 'gy', 'gx')
The draws below stay inside these ranges and needn't reach their ends.
Inputs may be any that keep to these rules, and one draw needn't show every extreme that they name: `populations`: every entry is positive, between 0.4 and 1.9 times its velocity's weight. `node_type`: cells of the first and last planes across the span and along the depth are walls, as are scattered obstacle cells; the other cells of the first plane along the stream are inlets, of the last plane outlets.
All inputs are finite; a program needn't handle non-finite values.
Results may differ from the reference program's by a relative error of at most 0.0001.
Values sent between devices are 32-bit elements; how exact they have to be, the bound alone decides.
A program may use at most 64 MiB of HBM per device.

```python
import math
import jax
import jax.numpy as jnp
from jax import lax

Q = 19
STEPS = 2
NX = 512
NY = 16
NZ = 16


lattice_velocities = ((0, 0, 0), (1, 0, 0), (-1, 0, 0), (0, 1, 0), (0, -1, 0), (0, 0, 1), (0, 0, -1), (1, 1, 0), (-1, -1, 0), (1, -1, 0), (-1, 1, 0), (1, 0, 1), (-1, 0, -1), (1, 0, -1), (-1, 0, 1), (0, 1, 1), (0, -1, -1), (0, 1, -1), (0, -1, 1))


lattice_weights = (1.0 / 3.0,) + (1.0 / 18.0,) * 6 + (1.0 / 36.0,) * 12


def draw_populations(key, part):
    key = jax.random.fold_in(key, 11)
    column_east = jnp.asarray([vector[0] for vector in lattice_velocities], jnp.float32)[:, None, None, None]
    weight_column = jnp.asarray(lattice_weights, jnp.float32)[:, None, None, None]
    projected = 0.1 * column_east
    baseline = weight_column * (1.0 + 3.0 * projected + 4.5 * projected * projected - 0.015)
    factor = jax.random.uniform(key, (Q, NZ, NY, NX), jnp.float32, 2.0 / 3.0, 4.0 / 3.0)
    return (baseline * factor).astype(jnp.float32)


def draw_node_type(key, part):
    key = jax.random.fold_in(key, 23)
    depth_pos = jnp.arange(NZ)[:, None, None]
    span_pos = jnp.arange(NY)[None, :, None]
    stream_pos = jnp.arange(NX)[None, None, :]
    obstacle = jax.random.randint(key, (NZ, NY, NX), 0, 10) == 0
    walled = (span_pos == 0) | (span_pos == NY - 1) | (depth_pos == 0) | (depth_pos == NZ - 1) | obstacle
    inlet_plane = (stream_pos == 0) & (span_pos == 1) | (stream_pos == 0)
    outlet_plane = stream_pos == NX - 1
    kinds = jnp.where(walled, 1, jnp.where(inlet_plane, 2, jnp.where(outlet_plane, 3, 0)))
    kinds = jnp.where((depth_pos == 1) & (span_pos == 1) & outlet_plane, 3, kinds)
    return kinds.astype(jnp.int32)


def block_levels(own_key, shape, shards, least, largest):
    factor_of, own = 1.0, jax.random.fold_in(own_key, 6)
    for position, blocks in shards:
        draws = jnp.exp(jax.random.uniform(jax.random.fold_in(own, position), (blocks,), jnp.float32, least / len(shards), largest / len(shards)))
        factor_of = factor_of * jnp.repeat(draws, shape[position] // blocks).reshape([-1 if axis == position else 1 for axis in range(len(shape))])
    return factor_of


def normal_values(key, extent, deviation, bound, cuts=(), held_as=jnp.bfloat16):
    values = jax.random.normal(key, extent, jnp.float32) * deviation
    if len(cuts) > 0:
        values = block_levels(key, extent, cuts, -0.22, 0.18) * values
    return jnp.clip(values, min=-bound, max=bound).astype(held_as)


def setup_inputs(seed: int = 0) -> dict:
    streams_of = jax.random.split(jax.random.key(seed), 6)
    return {
        "populations": draw_populations(jax.random.fold_in(streams_of[5], 71), 0),
        "porosity": jnp.clip(1.0 * jax.random.uniform(streams_of[1], (NZ, NY, NX), jnp.float32) ** block_levels(streams_of[1], (NZ, NY, NX), ((0, 4), (1, 2), (2, 4)), -0.2, 0.2), 0.0, 1.0),
        "node_type": draw_node_type(jax.random.fold_in(streams_of[5], 71), 0),
        "step_index": jax.random.randint(streams_of[3], (1,), 0, 4096).astype(jnp.int32),
        "adjoint_end": normal_values(streams_of[4], (Q, NZ, NY, NX), 1.0, 6.0, ((1, 4), (2, 2), (3, 4)), jnp.float32),
    }


lattice_velocities = ((0, 0, 0), (1, 0, 0), (-1, 0, 0), (0, 1, 0), (0, -1, 0), (0, 0, 1), (0, 0, -1), (1, 1, 0), (-1, -1, 0), (1, -1, 0), (-1, 1, 0), (1, 0, 1), (-1, 0, -1), (1, 0, -1), (-1, 0, 1), (0, 1, 1), (0, -1, -1), (0, 1, -1), (0, -1, 1))
lattice_weights = (1.0 / 3.0,) + (1.0 / 18.0,) * 6 + (1.0 / 36.0,) * 12
opposite_index = (0, 2, 1, 4, 3, 6, 5, 8, 7, 10, 9, 12, 11, 14, 13, 16, 15, 18, 17)
relax_rate = 1.25
ramp_factor = 0.1
inlet_base = 0.1
inlet_period = 64.0

def lattice_column(which):
    return jnp.asarray([vector[which] for vector in lattice_velocities], jnp.float32)[:, None, None, None]

def weight_column():
    return jnp.asarray(lattice_weights, jnp.float32)[:, None, None, None]

def equilibrium(density, flow_east, flow_north, flow_depth):
    projected = lattice_column(0) * flow_east + lattice_column(1) * flow_north + lattice_column(2) * flow_depth
    square = flow_east * flow_east + flow_north * flow_north + flow_depth * flow_depth
    return weight_column() * density * (1.0 + 3.0 * projected + 4.5 * projected * projected - 1.5 * square)

def collide(current, porosity, node_kinds, inlet_speed):
    density = lax.optimization_barrier(jnp.sum(current, axis=0))
    flow_east = lax.optimization_barrier(jnp.sum(lattice_column(0) * current, axis=0)) / density
    flow_north = lax.optimization_barrier(jnp.sum(lattice_column(1) * current, axis=0)) / density
    flow_depth = lax.optimization_barrier(jnp.sum(lattice_column(2) * current, axis=0)) / density
    damping = ramp_factor * (1.0 - porosity) / (ramp_factor + porosity)
    retained = 1.0 - damping
    relaxed = current - relax_rate * (current - equilibrium(density, retained * flow_east, retained * flow_north, retained * flow_depth))
    bounced = current[jnp.asarray(opposite_index)]
    unit_field = jnp.ones_like(density)
    inflow = equilibrium(unit_field, inlet_speed * unit_field, 0.0 * unit_field, 0.0 * unit_field)
    outflow = equilibrium(density, flow_east, flow_north, flow_depth)
    collided = jnp.where(node_kinds == 1, bounced, jnp.where(node_kinds == 2, inflow, jnp.where(node_kinds == 3, outflow, relaxed)))
    kinetic = flow_east * flow_east + flow_north * flow_north + flow_depth * flow_depth
    energy = jnp.where(node_kinds == 0, damping * density * kinetic, 0.0 * density)
    return (collided, energy)

def inlet_value(step_index, offset):
    moment = (step_index[0] + offset).astype(jnp.float32)
    return inlet_base * (1.0 + 0.8 * jnp.sin(2.0 * math.pi * moment / inlet_period))

def stream_periodic(field, sign):
    slabs = []
    for q in range(len(lattice_velocities)):
        vector = lattice_velocities[q]
        slabs.append(jnp.roll(field[q], (sign * vector[2], sign * vector[1], sign * vector[0]), axis=(0, 1, 2)))
    return jnp.stack(slabs)

def reference(populations, porosity, node_type, step_index, adjoint_end):
    states = []
    current = populations
    for t in range(STEPS):
        states.append(current)
        if t + 1 < STEPS:
            collided, energy = collide(current, porosity, node_type, inlet_value(step_index, t))
            current = stream_periodic(collided, 1)
    adjoint = adjoint_end
    sensitivity = jnp.zeros_like(porosity)
    for t in reversed(range(STEPS)):
        arriving = stream_periodic(adjoint, -1)
        inlet_speed = inlet_value(step_index, t)

        def local_step(incoming, design):
            return collide(incoming, design, node_type, inlet_speed)
        collided, pullback = jax.vjp(local_step, states[t], porosity)
        adjoint, design_grad = pullback((arriving, jnp.ones_like(porosity)))
        sensitivity = sensitivity + design_grad
    return (adjoint, sensitivity)
```

```python
import functools
import math

import jax
import jax.numpy as jnp
from jax import lax
from jax.experimental import pallas as pl
from jax.experimental.pallas import tpu as pltpu
from jax.sharding import PartitionSpec as P

MESH = pl.DeviceIdType.MESH

VEL = (
    (0, 0, 0),
    (1, 0, 0),
    (-1, 0, 0),
    (0, 1, 0),
    (0, -1, 0),
    (0, 0, 1),
    (0, 0, -1),
    (1, 1, 0),
    (-1, -1, 0),
    (1, -1, 0),
    (-1, 1, 0),
    (1, 0, 1),
    (-1, 0, -1),
    (1, 0, -1),
    (-1, 0, 1),
    (0, 1, 1),
    (0, -1, -1),
    (0, 1, -1),
    (0, -1, 1),
)
Q = len(VEL)
WEIGHT = (1.0 / 3.0,) + (1.0 / 18.0,) * 6 + (1.0 / 36.0,) * 12
OPP = (0, 2, 1, 4, 3, 6, 5, 8, 7, 10, 9, 12, 11, 14, 13, 16, 15, 18, 17)
SIGNS = (1, -1)


def side(move):
    return 0 if move == 1 else 1


def moves(sign):
    return [tuple(sign * c for c in v) for v in VEL]


def order_along(which, sign):
    place = {}
    for way in SIGNS:
        count = 0
        for q, m in enumerate(moves(sign)):
            if m[which] == way:
                place[q] = count
                count += 1
    return place


def message_list(merge):
    out = []
    ys = (1,) if merge else SIGNS
    for ox in SIGNS:
        for oz in SIGNS:
            out.append(((ox, 0, oz), "x", (side(ox), 3 + side(oz))))
    for oz in SIGNS:
        for oy in ys:
            out.append(((0, oy, oz), "e", (side(oy), side(oz))))
    for ox in SIGNS:
        for oy in ys:
            out.append(((ox, oy, 0), "x", (side(ox), 1 + side(oy))))
    for oz in SIGNS:
        out.append(((0, 0, oz), "z", (side(oz),)))
    if merge:
        out.append(((0, 1, 0), "yy", ()))
    else:
        for oy in SIGNS:
            out.append(((0, oy, 0), "y", (side(oy),)))
    for ox in SIGNS:
        out.append(((ox, 0, 0), "x", (side(ox), 0)))
    return out


def total(items):
    items = list(items)
    while len(items) > 1:
        nxt = [items[i] + items[i + 1] for i in range(0, len(items) - 1, 2)]
        if len(items) % 2:
            nxt.append(items[-1])
        items = nxt
    return items[0]


def first_moments(f):
    density = total(f)
    flow = []
    for d in range(3):
        plus = total([f[q] for q in range(Q) if VEL[q][d] == 1])
        minus = total([f[q] for q in range(Q) if VEL[q][d] == -1])
        flow.append(plus - minus)
    return density, flow


def along(b):
    bx, by, bz = b
    return {
        1: bx, 3: by, 5: bz,
        7: bx + by, 9: bx - by, 11: bx + bz, 13: bx - bz, 15: by + bz, 17: by - bz,
    }


def collided(f, r, v, alpha, wall):
    vv = v[0] * v[0] + v[1] * v[1] + v[2] * v[2]
    base = 1.0 - 1.5 * vv
    out = [None] * Q
    out[0] = jnp.where(wall, f[0], alpha * f[0] + (WEIGHT[0] * r) * base)
    by_weight = {1: WEIGHT[1] * r, 2: WEIGHT[7] * r}
    for q, cv in along(v).items():
        wr = by_weight[1 if q < 7 else 2]
        even = wr * (base + 4.5 * (cv * cv))
        odd = wr * (3.0 * cv)
        out[q] = jnp.where(wall, f[q + 1], alpha * f[q] + (even + odd))
        out[q + 1] = jnp.where(wall, f[q], alpha * f[q + 1] + (even - odd))
    return out


def pulled_back(g, r, u, cells):
    alpha, beta, keep, damp, wall = cells
    v = [keep * x for x in u]
    sums = {q: g[q] + g[q + 1] for q in range(1, Q, 2)}
    diff = {q: g[q] - g[q + 1] for q in range(1, Q, 2)}
    wa, wb = WEIGHT[1], WEIGHT[7]
    axes = total([sums[1], sums[3], sums[5]])
    diag = total([sums[q] for q in (7, 9, 11, 13, 15, 17)])
    g0 = WEIGHT[0] * g[0] + wa * axes + wb * diag
    gx = wa * diff[1] + wb * ((diff[7] + diff[9]) + (diff[11] + diff[13]))
    gy = wa * diff[3] + wb * ((diff[7] - diff[9]) + (diff[15] + diff[17]))
    gz = wa * diff[5] + wb * ((diff[11] - diff[13]) + (diff[15] - diff[17]))
    xy, xz, yz = sums[7] + sums[9], sums[11] + sums[13], sums[15] + sums[17]
    gxx = wa * sums[1] + wb * (xy + xz)
    gyy = wa * sums[3] + wb * (xy + yz)
    gzz = wa * sums[5] + wb * (xz + yz)
    gxy = wb * (sums[7] - sums[9])
    gxz = wb * (sums[11] - sums[13])
    gyz = wb * (sums[15] - sums[17])
    hx = 4.5 * (gxx * v[0] + gxy * v[1] + gxz * v[2]) - 1.5 * g0 * v[0]
    hy = 4.5 * (gxy * v[0] + gyy * v[1] + gyz * v[2]) - 1.5 * g0 * v[1]
    hz = 4.5 * (gxz * v[0] + gyz * v[1] + gzz * v[2]) - 1.5 * g0 * v[2]
    slope = [3.0 * gx + 2.0 * hx, 3.0 * gy + 2.0 * hy, 3.0 * gz + 2.0 * hz]
    quad = v[0] * hx + v[1] * hy + v[2] * hz
    uu = u[0] * u[0] + u[1] * u[1] + u[2] * u[2]
    a0 = beta * (g0 - quad) - damp * uu
    scale = beta * keep
    twice = 2.0 * damp
    b = [scale * s + twice * x for s, x in zip(slope, u)]
    out = [None] * Q
    out[0] = jnp.where(wall, g[0], alpha * g[0] + a0)
    for q, cb in along(b).items():
        out[q] = jnp.where(wall, g[q + 1], alpha * g[q] + (a0 + cb))
        out[q + 1] = jnp.where(wall, g[q], alpha * g[q + 1] + (a0 - cb))
    by_damp = r * (uu - 1.25 * (slope[0] * u[0] + slope[1] * u[1] + slope[2] * u[2]))
    return out, by_damp


class Exchange:
    def __init__(self, signs, nz, refs):
        self.signs = signs
        self.nz = nz
        self.kept, self.px, self.py, self.pe, self.pz = refs[:5]
        self.rx, self.ry, self.re, self.rz = refs[5:]
        self.count = 5 * nz
        self.lane = lax.broadcasted_iota(jnp.int32, (8, 128), 1)
        self.row = lax.broadcasted_iota(jnp.int32, (8, 128), 0)
        zero = jnp.zeros((8, 128), jnp.float32)
        self.packed = [zero, zero]
        self.moves = [moves(s) for s in signs]
        self.places = [[order_along(d, s) for d in range(3)] for s in signs]

    def edge_row(self, fi, oy, oz):
        return (fi * 2 + side(oy)) * 2 + side(oz)

    def scatter(self, fi, z, tiles):
        nz = self.nz
        for q in range(Q):
            mx, my, mz = self.moves[fi][q]
            place = self.places[fi]
            t = tiles[q]
            if my:
                t = pltpu.roll(t, my % 8, axis=0)
            flat = t
            if mx:
                t = pltpu.roll(t, mx % 128, axis=1)
            zp = (z + mz) % nz
            wraps = zp != z + mz
            if wraps:
                self.pz[side(mz), fi * 5 + place[2][q]] = t
            else:
                self.kept[fi, q, zp] = t
            if mx:
                k = fi * self.count + place[0][q] * nz + zp
                moved = pltpu.roll(flat, (k + 1 if mx == 1 else k + 1 + 127) % 128, axis=1) \
                    if mx == 1 else pltpu.roll(flat, k % 128, axis=1) if k else flat
                s = side(mx)
                self.packed[s] = jnp.where(self.lane == k, moved, self.packed[s])
            if my:
                w = 0 if my == 1 else 7
                s = side(my)
                edge = t[w : w + 1, :]
                if wraps:
                    e = self.edge_row(fi, my, mz)
                    self.pe[e : e + 1, :] = edge
                else:
                    k = fi * self.count + place[1][q] * nz + zp
                    self.py[s, k : k + 1, :] = edge

    def pack(self):
        for s in (0, 1):
            self.px[s] = self.packed[s]

    def gather(self, fi, z, merge):
        nz = self.nz
        out = []
        for q in range(Q):
            mx, my, mz = self.moves[fi][q]
            place = self.places[fi]
            wraps = (mz == 1 and z == 0) or (mz == -1 and z == nz - 1)
            if wraps:
                t = self.rz[side(mz), fi * 5 + place[2][q]]
            else:
                t = self.kept[fi, q, z]
            sy = 0 if merge else side(my)
            w = 0 if my == 1 else 7
            if my:
                if wraps:
                    e = self.edge_row(fi, my, mz)
                    edge = self.re[sy, side(mz), e : e + 1, :]
                else:
                    k = fi * self.count + place[1][q] * nz + z
                    edge = self.ry[side(my), k : k + 1, :]
                t = jnp.where(self.row == w, jnp.broadcast_to(edge, (8, 128)), t)
            if mx:
                s = side(mx)
                k = fi * self.count + place[0][q] * nz + z
                if wraps:
                    col = self.rx[s, 3 + side(mz)]
                else:
                    col = self.rx[s, 0]
                    if my:
                        col = jnp.where(self.row == w, self.rx[s, 1 + sy], col)
                target = 0 if mx == 1 else 127
                shift = (target - k) % 128
                if shift:
                    col = pltpu.roll(col, shift, axis=1)
                t = jnp.where(self.lane == target, col, t)
            out.append(t)
        return out


def kernel(
    sizes, nz,
    step_ref, pop_hbm, por_hbm, kind_hbm, adj_hbm,
    out_ref, sens_ref,
    pop, por, kind, adj, saved, load_sem,
    kept1, px1, py1, pe1, pz1, rx1, ry1, re1, rz1,
    kept2, px2, py2, pe2, pz2, rx2, ry2, re2, rz2,
    send1, recv1, send2, recv2,
):
    merge = sizes[1] == 2
    names = ("gx", "gy", "gz")
    here = [lax.axis_index(n) for n in names]
    messages = message_list(merge)

    def target(offset):
        return {
            n: lax.rem(here[d] + (offset[d] + sizes[d]), sizes[d])
            for d, n in enumerate(names) if offset[d]
        }

    loads = [
        pltpu.make_async_copy(src, dst, load_sem.at[i])
        for i, (src, dst) in enumerate(
            ((adj_hbm, adj), (pop_hbm, pop), (por_hbm, por), (kind_hbm, kind))
        )
    ]
    for c in loads:
        c.start()
    barrier = pltpu.get_barrier_semaphore()
    for offset, _, _ in messages:
        pl.semaphore_signal(barrier, inc=1, device_id=target(offset), device_id_type=MESH)

    def copies(bufs, send, recv):
        px, py, pe, pz, rx, ry, re, rz = bufs
        made = []
        for i, (offset, what, at) in enumerate(messages):
            if what == "x":
                src, dst = px.at[at[0]], rx.at[at[0], at[1]]
            elif what == "e":
                src, dst = pe, re.at[at[0], at[1]]
            elif what == "z":
                src, dst = pz.at[at[0]], rz.at[at[0]]
            elif what == "yy":
                src, dst = py, ry
            else:
                src, dst = py.at[at[0]], ry.at[at[0]]
            made.append(pltpu.make_async_remote_copy(
                src_ref=src, dst_ref=dst, send_sem=send.at[i], recv_sem=recv.at[i],
                device_id=target(offset), device_id_type=MESH,
            ))
        return made

    first = Exchange((1, -1), nz, (kept1, px1, py1, pe1, pz1, rx1, ry1, re1, rz1))
    second = Exchange((-1,), nz, (kept2, px2, py2, pe2, pz2, rx2, ry2, re2, rz2))

    pe1[...] = jnp.zeros_like(pe1)
    py1[...] = jnp.zeros_like(py1)
    pe2[...] = jnp.zeros_like(pe2)
    py2[...] = jnp.zeros_like(py2)

    loads[0].wait()
    for z in range(nz):
        first.scatter(1, z, [adj[q, z] for q in range(Q)])

    moment = jnp.full((8, 128), jnp.bitwise_and(step_ref[0], 63), jnp.int32)
    angle = moment.astype(jnp.float32) * (2.0 * math.pi / 64.0)
    inlet_speed = 0.1 * (1.0 + 0.8 * jnp.sin(angle))
    zero = jnp.zeros((8, 128), jnp.float32)

    def cell_kinds(z):
        n = kind[z]
        fluid = n == 0
        outlet = n == 3
        denom = 0.1 + por[z]
        k = 0.1 * (1.0 - por[z]) / denom
        alpha = jnp.where(fluid, -0.25, 0.0)
        beta = jnp.where(fluid, 1.25, jnp.where(outlet, 1.0, 0.0))
        keep = jnp.where(fluid, 1.0 - k, 1.0)
        damp = jnp.where(fluid, k, 0.0)
        return n, (alpha, beta, keep, damp, n == 1), denom

    for c in loads[1:]:
        c.wait()
    for z in range(nz):
        n, cells, denom = cell_kinds(z)
        alpha, beta, keep, damp, wall = cells
        f = [pop[q, z] for q in range(Q)]
        r, flow = first_moments(f)
        u = [m / r for m in flow]
        inlet = n == 2
        v = [
            jnp.where(inlet, inlet_speed, keep * u[0]),
            jnp.where(inlet, zero, keep * u[1]),
            jnp.where(inlet, zero, keep * u[2]),
        ]
        first.scatter(0, z, collided(f, jnp.where(inlet, 1.0, beta * r), v, alpha, wall))
        saved[z, 0] = r
        for d in range(3):
            saved[z, 1 + d] = u[d]
        saved[z, 4] = keep
        saved[z, 5] = damp
        saved[z, 6] = jnp.where(n == 0, -0.11 / (denom * denom), 0.0)
    first.pack()
    pl.semaphore_wait(barrier, len(messages))
    sent1 = copies((px1, py1, pe1, pz1, rx1, ry1, re1, rz1), send1, recv1)
    for c in sent1:
        c.start()
    for c in sent1:
        c.wait_recv()

    def saved_cells(z):
        n = kind[z]
        fluid = n == 0
        alpha = jnp.where(fluid, -0.25, 0.0)
        beta = jnp.where(fluid, 1.25, jnp.where(n == 3, 1.0, 0.0))
        return alpha, beta, saved[z, 4], saved[z, 5], n == 1

    for z in range(nz):
        r, flow = first_moments(first.gather(0, z, merge))
        u = [m / r for m in flow]
        a, by_damp = pulled_back(first.gather(1, z, merge), r, u, saved_cells(z))
        sens_ref[z] = by_damp
        second.scatter(0, z, a)
    second.pack()
    sent2 = copies((px2, py2, pe2, pz2, rx2, ry2, re2, rz2), send2, recv2)
    for c in sent2:
        c.start()
    for c in sent2:
        c.wait_recv()
    for z in range(nz):
        u = [saved[z, 1 + d] for d in range(3)]
        a, by_damp = pulled_back(second.gather(0, z, merge), saved[z, 0], u, saved_cells(z))
        sens_ref[z] = saved[z, 6] * (sens_ref[z] + by_damp)
        for q in range(Q):
            out_ref[q, z] = a[q]
    for c in sent1:
        c.wait_send()
    for c in sent2:
        c.wait_send()


def buffers(fields, nz):
    rows = -(-fields * 5 * nz // 8) * 8
    f32 = jnp.float32
    return [
        pltpu.VMEM((fields, Q, nz, 8, 128), f32),
        pltpu.VMEM((2, 8, 128), f32),
        pltpu.VMEM((2, rows, 128), f32),
        pltpu.VMEM((8, 128), f32),
        pltpu.VMEM((2, fields * 5, 8, 128), f32),
        pltpu.VMEM((2, 5, 8, 128), f32),
        pltpu.VMEM((2, rows, 128), f32),
        pltpu.VMEM((2, 2, 8, 128), f32),
        pltpu.VMEM((2, fields * 5, 8, 128), f32),
    ]


def on_device(sizes, populations, porosity, node_type, step_index, adjoint_end):
    _, nz, ny, nx = populations.shape
    assert (ny, nx) == (8, 128) and 10 * nz <= 128
    f32 = jnp.float32
    count = len(message_list(sizes[1] == 2))
    any_space = pl.BlockSpec(memory_space=pl.ANY)
    vmem = pl.BlockSpec(memory_space=pltpu.VMEM)
    return pl.pallas_call(
        functools.partial(kernel, sizes, nz),
        out_shape=(
            jax.ShapeDtypeStruct(populations.shape, f32),
            jax.ShapeDtypeStruct(porosity.shape, f32),
        ),
        in_specs=[pl.BlockSpec(memory_space=pltpu.SMEM)] + [any_space] * 4,
        out_specs=(vmem, vmem),
        scratch_shapes=[
            pltpu.VMEM(populations.shape, f32),
            pltpu.VMEM(porosity.shape, f32),
            pltpu.VMEM(node_type.shape, jnp.int32),
            pltpu.VMEM(populations.shape, f32),
            pltpu.VMEM((nz, 7, 8, 128), f32),
            pltpu.SemaphoreType.DMA((4,)),
        ] + buffers(2, nz) + buffers(1, nz) + [pltpu.SemaphoreType.DMA((count,))] * 4,
        compiler_params=pltpu.CompilerParams(collective_id=0, has_side_effects=True),
    )(step_index, populations, porosity, node_type, adjoint_end)


def solution(mesh):
    sizes = tuple(mesh.shape[n] for n in ("gx", "gy", "gz"))
    return jax.shard_map(
        functools.partial(on_device, sizes),
        mesh=mesh,
        in_specs=(
            P(None, "gz", "gy", "gx"),
            P("gz", "gy", "gx"),
            P("gz", "gy", "gx"),
            P(),
            P(None, "gz", "gy", "gx"),
        ),
        out_specs=(P(None, "gz", "gy", "gx"), P("gz", "gy", "gx")),
        check_vma=False,
    )
```

```python
import functools
import math

import jax
import jax.numpy as jnp
from jax import lax
from jax.experimental import pallas as pl
from jax.experimental.pallas import tpu as pltpu
from jax.sharding import PartitionSpec as P

MESH = pl.DeviceIdType.MESH

VEL = (
    (0, 0, 0),
    (1, 0, 0),
    (-1, 0, 0),
    (0, 1, 0),
    (0, -1, 0),
    (0, 0, 1),
    (0, 0, -1),
    (1, 1, 0),
    (-1, -1, 0),
    (1, -1, 0),
    (-1, 1, 0),
    (1, 0, 1),
    (-1, 0, -1),
    (1, 0, -1),
    (-1, 0, 1),
    (0, 1, 1),
    (0, -1, -1),
    (0, 1, -1),
    (0, -1, 1),
)
Q = len(VEL)
WEIGHT = (1.0 / 3.0,) + (1.0 / 18.0,) * 6 + (1.0 / 36.0,) * 12
OPP = (0, 2, 1, 4, 3, 6, 5, 8, 7, 10, 9, 12, 11, 14, 13, 16, 15, 18, 17)
SIGNS = (1, -1)


def side(move):
    return 0 if move == 1 else 1


def moves(sign):
    return [tuple(sign * c for c in v) for v in VEL]


def order_along(which, sign):
    place = {}
    for way in SIGNS:
        count = 0
        for q, m in enumerate(moves(sign)):
            if m[which] == way:
                place[q] = count
                count += 1
    return place


def message_list(merge):
    ys = (1,) if merge else SIGNS
    out = []
    for oz in SIGNS:
        out += [((ox, 0, oz), "xz", (side(ox), 3 + side(oz))) for ox in SIGNS]
        out += [((0, oy, oz), "e", (side(oy), side(oz))) for oy in ys]
        out.append(((0, 0, oz), "z", (side(oz),)))
    for ox in SIGNS:
        out += [((ox, oy, 0), "x", (side(ox), 1 + side(oy))) for oy in ys]
    out += [((0, oy, 0), "yy" if merge else "y", (side(oy),)) for oy in ys]
    out += [((ox, 0, 0), "x", (side(ox), 0)) for ox in SIGNS]
    return out


EARLY = ("xz", "e", "z")


def total(items):
    items = list(items)
    while len(items) > 1:
        nxt = [items[i] + items[i + 1] for i in range(0, len(items) - 1, 2)]
        if len(items) % 2:
            nxt.append(items[-1])
        items = nxt
    return items[0]


def first_moments(f):
    density = total(f)
    flow = []
    for d in range(3):
        plus = total([f[q] for q in range(Q) if VEL[q][d] == 1])
        minus = total([f[q] for q in range(Q) if VEL[q][d] == -1])
        flow.append(plus - minus)
    return density, flow


def along(b):
    bx, by, bz = b
    return {
        1: bx, 3: by, 5: bz,
        7: bx + by, 9: bx - by, 11: bx + bz, 13: bx - bz, 15: by + bz, 17: by - bz,
    }


def collided(f, r, v, alpha, wall):
    vv = v[0] * v[0] + v[1] * v[1] + v[2] * v[2]
    base = 1.0 - 1.5 * vv
    out = [None] * Q
    out[0] = jnp.where(wall, f[0], alpha * f[0] + (WEIGHT[0] * r) * base)
    by_weight = {1: WEIGHT[1] * r, 2: WEIGHT[7] * r}
    for q, cv in along(v).items():
        wr = by_weight[1 if q < 7 else 2]
        even = wr * (base + 4.5 * (cv * cv))
        odd = wr * (3.0 * cv)
        out[q] = jnp.where(wall, f[q + 1], alpha * f[q] + (even + odd))
        out[q + 1] = jnp.where(wall, f[q], alpha * f[q + 1] + (even - odd))
    return out


def pulled_back(g, r, u, cells):
    alpha, beta, keep, damp, wall = cells
    v = [keep * x for x in u]
    sums = {q: g[q] + g[q + 1] for q in range(1, Q, 2)}
    diff = {q: g[q] - g[q + 1] for q in range(1, Q, 2)}
    wa, wb = WEIGHT[1], WEIGHT[7]
    axes = total([sums[1], sums[3], sums[5]])
    diag = total([sums[q] for q in (7, 9, 11, 13, 15, 17)])
    g0 = WEIGHT[0] * g[0] + wa * axes + wb * diag
    gx = wa * diff[1] + wb * ((diff[7] + diff[9]) + (diff[11] + diff[13]))
    gy = wa * diff[3] + wb * ((diff[7] - diff[9]) + (diff[15] + diff[17]))
    gz = wa * diff[5] + wb * ((diff[11] - diff[13]) + (diff[15] - diff[17]))
    xy, xz, yz = sums[7] + sums[9], sums[11] + sums[13], sums[15] + sums[17]
    gxx = wa * sums[1] + wb * (xy + xz)
    gyy = wa * sums[3] + wb * (xy + yz)
    gzz = wa * sums[5] + wb * (xz + yz)
    gxy = wb * (sums[7] - sums[9])
    gxz = wb * (sums[11] - sums[13])
    gyz = wb * (sums[15] - sums[17])
    hx = 4.5 * (gxx * v[0] + gxy * v[1] + gxz * v[2]) - 1.5 * g0 * v[0]
    hy = 4.5 * (gxy * v[0] + gyy * v[1] + gyz * v[2]) - 1.5 * g0 * v[1]
    hz = 4.5 * (gxz * v[0] + gyz * v[1] + gzz * v[2]) - 1.5 * g0 * v[2]
    slope = [3.0 * gx + 2.0 * hx, 3.0 * gy + 2.0 * hy, 3.0 * gz + 2.0 * hz]
    quad = v[0] * hx + v[1] * hy + v[2] * hz
    uu = u[0] * u[0] + u[1] * u[1] + u[2] * u[2]
    a0 = beta * (g0 - quad) - damp * uu
    scale = beta * keep
    twice = 2.0 * damp
    b = [scale * s + twice * x for s, x in zip(slope, u)]
    out = [None] * Q
    out[0] = jnp.where(wall, g[0], alpha * g[0] + a0)
    for q, cb in along(b).items():
        out[q] = jnp.where(wall, g[q + 1], alpha * g[q] + (a0 + cb))
        out[q + 1] = jnp.where(wall, g[q], alpha * g[q + 1] + (a0 - cb))
    by_damp = r * (uu - 1.25 * (slope[0] * u[0] + slope[1] * u[1] + slope[2] * u[2]))
    return out, by_damp


class Exchange:
    def __init__(self, signs, nz, refs):
        self.signs = signs
        self.nz = nz
        self.px, self.pq, self.py, self.pe, self.pz = refs[:5]
        self.kept, self.rx, self.ry, self.re, self.rz = refs[5:]
        self.count = 5 * nz
        self.lane = lax.broadcasted_iota(jnp.int32, (8, 128), 1)
        self.row = lax.broadcasted_iota(jnp.int32, (8, 128), 0)
        zero = jnp.zeros((8, 128), jnp.float32)
        self.packed = [zero, zero]
        self.moves = [moves(s) for s in signs]
        self.places = [[order_along(d, s) for d in range(3)] for s in signs]

    def edge_row(self, fi, oy, oz):
        return (fi * 2 + side(oy)) * 2 + side(oz)

    def scatter(self, fi, z, tiles):
        nz = self.nz
        for q in range(Q):
            mx, my, mz = self.moves[fi][q]
            place = self.places[fi]
            t = tiles[q]
            if my:
                t = pltpu.roll(t, my % 8, axis=0)
            flat = t
            if mx:
                t = pltpu.roll(t, mx % 128, axis=1)
            zp = (z + mz) % nz
            wraps = zp != z + mz
            if wraps:
                self.pz[side(mz), fi * 5 + place[2][q]] = t
            else:
                self.kept[fi, q, zp] = t
            if mx:
                k = fi * self.count + place[0][q] * nz + zp
                shift = k + 1 if mx == 1 else k
                moved = pltpu.roll(flat, shift, axis=1) if shift else flat
                s = side(mx)
                self.packed[s] = jnp.where(self.lane == k, moved, self.packed[s])
            if my:
                w = 0 if my == 1 else 7
                s = side(my)
                edge = t[w : w + 1, :]
                if wraps:
                    e = self.edge_row(fi, my, mz)
                    self.pe[e : e + 1, :] = edge
                else:
                    k = fi * self.count + place[1][q] * nz + zp
                    self.py[s, k : k + 1, :] = edge

    def pack(self, target):
        for s in (0, 1):
            target[s] = self.packed[s]

    def gather(self, fi, z, merge, given=None):
        nz = self.nz
        out = []
        for q in range(Q):
            mx, my, mz = self.moves[fi][q]
            place = self.places[fi]
            wraps = (mz == 1 and z == 0) or (mz == -1 and z == nz - 1)
            if wraps:
                t = self.rz[side(mz), fi * 5 + place[2][q]]
            else:
                t = self.kept[fi, q, z]
            sy = 0 if merge else side(my)
            w = 0 if my == 1 else 7
            if my:
                if wraps:
                    e = self.edge_row(fi, my, mz)
                    edge = self.re[sy, side(mz), e : e + 1, :]
                else:
                    k = fi * self.count + place[1][q] * nz + z
                    edge = self.ry[side(my), k : k + 1, :]
                t = jnp.where(self.row == w, jnp.broadcast_to(edge, (8, 128)), t)
            if mx:
                s = side(mx)
                k = fi * self.count + place[0][q] * nz + z
                if wraps:
                    col = self.rx[s, 3 + side(mz)]
                else:
                    col = self.rx[s, 0]
                    if my:
                        col = jnp.where(self.row == w, self.rx[s, 1 + sy], col)
                target = 0 if mx == 1 else 127
                shift = (target - k) % 128
                if shift:
                    col = pltpu.roll(col, shift, axis=1)
                t = jnp.where(self.lane == target, col, t)
            if given is not None and (my or wraps):
                span, depth, tiles = given
                mask = None
                if my:
                    mask = jnp.logical_and(self.row == w, span)
                if wraps:
                    whole = depth[side(mz)]
                    mask = whole if mask is None else jnp.logical_or(mask, whole)
                t = jnp.where(mask, tiles(OPP[q]), t)
            out.append(t)
        return out


def saved_cells(saved, kind, z):
    n = kind[z]
    fluid = n == 0
    alpha = jnp.where(fluid, -0.25, 0.0)
    beta = jnp.where(fluid, 1.25, jnp.where(n == 3, 1.0, 0.0))
    return alpha, beta, saved[z, 4], saved[z, 5], n == 1


def depth_order(nz):
    return [0, nz - 1] + list(range(1, nz - 1))


def window(
    sizes, nz,
    step, pop_hbm, por_hbm, kind_hbm, adj_hbm,
    adj, kind, saved, part, edges, kept2, rx2, ry2, re2, rz2,
    pop, por, load_sem,
    px1, pq1, py1, pe1, pz1, px2, pq2, py2, pe2, pz2,
    kept1, rx1, ry1, re1, rz1,
    send1, recv1, send2, recv2,
):
    merge = sizes[1] == 2
    names = ("gx", "gy", "gz")
    here = [lax.axis_index(n) for n in names]
    messages = message_list(merge)

    loads = [
        pltpu.make_async_copy(src, dst, load_sem.at[i])
        for i, (src, dst) in enumerate(
            ((adj_hbm, adj), (pop_hbm, pop), (por_hbm, por), (kind_hbm, kind))
        )
    ]
    for c in loads:
        c.start()

    def target(offset):
        return {
            n: lax.rem(here[d] + (offset[d] + sizes[d]), sizes[d])
            for d, n in enumerate(names) if offset[d]
        }

    def inside(offset, way):
        ok = None
        for d in (1, 2):
            if offset[d] and not (d == 1 and merge):
                place = here[d] + way * offset[d]
                test = place < sizes[d] if way * offset[d] > 0 else place >= 0
                ok = test if ok is None else jnp.logical_and(ok, test)
        return ok

    def guarded(ok, act):
        if ok is None:
            act()
        else:
            pl.when(ok)(act)

    barrier = pltpu.get_barrier_semaphore()
    expected = 0
    for offset, _, _ in messages:
        guarded(inside(offset, 1), lambda offset=offset: pl.semaphore_signal(
            barrier, inc=1, device_id=target(offset), device_id_type=MESH))
        ok = inside(offset, -1)
        expected = expected + (1 if ok is None else jnp.where(ok, 1, 0))

    def copies(bufs, send, recv):
        px, pq, py, pe, pz, rx, ry, re, rz = bufs
        made = []
        for i, (offset, what, at) in enumerate(messages):
            if what == "x":
                src, dst = px.at[at[0]], rx.at[at[0], at[1]]
            elif what == "xz":
                src, dst = pq.at[at[0]], rx.at[at[0], at[1]]
            elif what == "e":
                src, dst = pe, re.at[at[0], at[1]]
            elif what == "z":
                src, dst = pz.at[at[0]], rz.at[at[0]]
            elif what == "yy":
                src, dst = py.at[here[1]], ry.at[here[1]]
            else:
                src, dst = py.at[at[0]], ry.at[at[0]]
            made.append((what in EARLY, offset, pltpu.make_async_remote_copy(
                src_ref=src, dst_ref=dst, send_sem=send.at[i], recv_sem=recv.at[i],
                device_id=target(offset), device_id_type=MESH,
            )))
        return made

    def start(made, early):
        for when, offset, c in made:
            if when == early:
                guarded(inside(offset, 1), c.start)

    def arrive(made):
        for _, offset, c in made:
            guarded(inside(offset, -1), c.wait_recv)

    def leave(made):
        for _, offset, c in made:
            guarded(inside(offset, 1), c.wait_send)

    first = Exchange((1, -1), nz, (px1, pq1, py1, pe1, pz1, kept1, rx1, ry1, re1, rz1))
    second = Exchange((-1,), nz, (px2, pq2, py2, pe2, pz2, kept2, rx2, ry2, re2, rz2))

    pe1[...] = jnp.zeros_like(pe1)
    py1[...] = jnp.zeros_like(py1)
    pe2[...] = jnp.zeros_like(pe2)
    py2[...] = jnp.zeros_like(py2)

    row = first.row
    span = jnp.logical_or(
        jnp.logical_and(row == 0, jnp.full((8, 128), here[1], jnp.int32) == 0),
        jnp.logical_and(row == 7, jnp.full((8, 128), here[1], jnp.int32) == sizes[1] - 1),
    )
    depth = jnp.full((8, 128), here[2], jnp.int32)
    edges[0] = jnp.where(span, 1, 0)
    edges[1] = jnp.where(depth == 0, 1, 0)
    edges[2] = jnp.where(depth == sizes[2] - 1, 1, 0)

    loads[0].wait()
    for z in depth_order(nz):
        first.scatter(1, z, [adj[q, z] for q in range(Q)])

    for c in loads[1:]:
        c.wait()
    moment = jnp.full((8, 128), jnp.bitwise_and(step[0], 63), jnp.int32)
    angle = moment.astype(jnp.float32) * (2.0 * math.pi / 64.0)
    inlet_speed = 0.1 * (1.0 + 0.8 * jnp.sin(angle))
    zero = jnp.zeros((8, 128), jnp.float32)

    sent1 = copies((px1, pq1, py1, pe1, pz1, rx1, ry1, re1, rz1), send1, recv1)
    sent2 = copies((px2, pq2, py2, pe2, pz2, rx2, ry2, re2, rz2), send2, recv2)
    for turn, z in enumerate(depth_order(nz)):
        n = kind[z]
        fluid = n == 0
        inlet = n == 2
        wall = n == 1
        denom = 0.1 + por[z]
        k = 0.1 * (1.0 - por[z]) / denom
        alpha = jnp.where(fluid, -0.25, 0.0)
        beta = jnp.where(fluid, 1.25, jnp.where(n == 3, 1.0, 0.0))
        keep = jnp.where(fluid, 1.0 - k, 1.0)
        f = [pop[q, z] for q in range(Q)]
        r, flow = first_moments(f)
        u = [m / r for m in flow]
        v = [
            jnp.where(inlet, inlet_speed, keep * u[0]),
            jnp.where(inlet, zero, keep * u[1]),
            jnp.where(inlet, zero, keep * u[2]),
        ]
        first.scatter(0, z, collided(f, jnp.where(inlet, 1.0, beta * r), v, alpha, wall))
        saved[z, 0] = r
        for d in range(3):
            saved[z, 1 + d] = u[d]
        saved[z, 4] = keep
        saved[z, 5] = jnp.where(fluid, k, 0.0)
        saved[z, 6] = -0.11 / (denom * denom)
        if turn == 1:
            first.pack(pq1)
            pl.semaphore_wait(barrier, expected)
            start(sent1, True)
    first.pack(px1)
    start(sent1, False)
    arrive(sent1)

    for turn, z in enumerate(depth_order(nz)):
        r, flow = first_moments(first.gather(0, z, merge))
        u = [m / r for m in flow]
        a, by_damp = pulled_back(
            first.gather(1, z, merge), r, u, saved_cells(saved, kind, z))
        part[z] = by_damp
        second.scatter(0, z, a)
        if turn == 1:
            second.pack(pq2)
            start(sent2, True)
    second.pack(px2)
    start(sent2, False)
    leave(sent1)
    arrive(sent2)
    leave(sent2)


def last_step(
    merge, nz,
    adj, kind, saved, part, edges, kept, rx, ry, re, rz,
    out_hbm, sens_hbm,
    out, sens, out_sem, sens_sem,
):
    field = Exchange((-1,), nz, (None,) * 5 + (kept, rx, ry, re, rz))
    span = edges[0] == 1
    depth = (edges[1] == 1, edges[2] == 1)
    copies = []
    for z in range(nz):
        g = field.gather(0, z, merge, (span, depth, lambda q, z=z: adj[q, z]))
        u = [saved[z, 1 + d] for d in range(3)]
        a, by_damp = pulled_back(g, saved[z, 0], u, saved_cells(saved, kind, z))
        sens[z] = jnp.where(kind[z] == 0, saved[z, 6] * (part[z] + by_damp), 0.0)
        for q in range(Q):
            out[q, z] = a[q]
        c = pltpu.make_async_copy(out.at[:, z], out_hbm.at[:, z], out_sem.at[z])
        c.start()
        copies.append(c)
    c = pltpu.make_async_copy(sens, sens_hbm, sens_sem)
    c.start()
    copies.append(c)
    for c in copies:
        c.wait()


def packed_shapes(fields, nz):
    rows = -(-fields * 5 * nz // 8) * 8
    return [
        (2, 8, 128), (2, 8, 128), (2, rows, 128), (8, 128), (2, fields * 5, 8, 128),
    ]


def landing_shapes(fields, nz):
    rows = -(-fields * 5 * nz // 8) * 8
    return [
        (fields, Q, nz, 8, 128), (2, 5, 8, 128), (2, rows, 128), (2, 2, 8, 128),
        (2, fields * 5, 8, 128),
    ]


LIMIT = 8 * 1024 * 1024


def on_device(sizes, populations, porosity, node_type, step_index, adjoint_end):
    _, nz, ny, nx = populations.shape
    assert (ny, nx) == (8, 128) and nz >= 2 and 10 * nz <= 128
    f32 = jnp.float32
    i32 = jnp.int32
    merge = sizes[1] == 2
    count = len(message_list(merge))
    any_space = pl.BlockSpec(memory_space=pl.ANY)
    vmem = pl.BlockSpec(memory_space=pltpu.VMEM)
    handed = [
        pltpu.VMEM(populations.shape, f32),
        pltpu.VMEM(node_type.shape, i32),
        pltpu.VMEM((nz, 7, 8, 128), f32),
        pltpu.VMEM(porosity.shape, f32),
        pltpu.VMEM((3, 8, 128), i32),
    ] + [pltpu.VMEM(s, f32) for s in landing_shapes(1, nz)]
    scratch = packed_shapes(2, nz) + packed_shapes(1, nz) + landing_shapes(2, nz)
    state = pl.pallas_call(
        functools.partial(window, sizes, nz),
        out_shape=handed,
        in_specs=[pl.BlockSpec(memory_space=pltpu.SMEM)] + [pl.BlockSpec(memory_space=pltpu.HBM)] * 4,
        out_specs=[vmem] * len(handed),
        scratch_shapes=[
            pltpu.VMEM(populations.shape, f32),
            pltpu.VMEM(porosity.shape, f32),
            pltpu.SemaphoreType.DMA((4,)),
        ] + [pltpu.VMEM(s, f32) for s in scratch] + [pltpu.SemaphoreType.DMA((count,))] * 4,
        compiler_params=pltpu.CompilerParams(
            collective_id=0, has_side_effects=True, vmem_limit_bytes=LIMIT),
    )(step_index, *[
        pltpu.with_memory_space_constraint(x, pltpu.HBM)
        for x in (populations, porosity, node_type, adjoint_end)
    ])
    return pl.pallas_call(
        functools.partial(last_step, merge, nz),
        out_shape=(
            jax.ShapeDtypeStruct(populations.shape, f32),
            jax.ShapeDtypeStruct(porosity.shape, f32),
        ),
        in_specs=[vmem] * len(handed),
        out_specs=(any_space, any_space),
        scratch_shapes=[
            pltpu.VMEM(populations.shape, f32),
            pltpu.VMEM(porosity.shape, f32),
            pltpu.SemaphoreType.DMA((nz,)),
            pltpu.SemaphoreType.DMA,
        ],
        compiler_params=pltpu.CompilerParams(vmem_limit_bytes=LIMIT),
    )(*state)


def solution(mesh):
    sizes = tuple(mesh.shape[n] for n in ("gx", "gy", "gz"))
    return jax.shard_map(
        functools.partial(on_device, sizes),
        mesh=mesh,
        in_specs=(
            P(None, "gz", "gy", "gx"),
            P("gz", "gy", "gx"),
            P("gz", "gy", "gx"),
            P(),
            P(None, "gz", "gy", "gx"),
        ),
        out_specs=(P(None, "gz", "gy", "gx"), P("gz", "gy", "gx")),
        check_vma=False,
    )
```

```python
import functools
import math

import jax
import jax.numpy as jnp
from jax import lax
from jax.experimental import pallas as pl
from jax.experimental.pallas import tpu as pltpu
from jax.sharding import PartitionSpec as P

MESH = pl.DeviceIdType.MESH

VEL = (
    (0, 0, 0),
    (1, 0, 0),
    (-1, 0, 0),
    (0, 1, 0),
    (0, -1, 0),
    (0, 0, 1),
    (0, 0, -1),
    (1, 1, 0),
    (-1, -1, 0),
    (1, -1, 0),
    (-1, 1, 0),
    (1, 0, 1),
    (-1, 0, -1),
    (1, 0, -1),
    (-1, 0, 1),
    (0, 1, 1),
    (0, -1, -1),
    (0, 1, -1),
    (0, -1, 1),
)
Q = len(VEL)
WEIGHT = (1.0 / 3.0,) + (1.0 / 18.0,) * 6 + (1.0 / 36.0,) * 12
OPP = (0, 2, 1, 4, 3, 6, 5, 8, 7, 10, 9, 12, 11, 14, 13, 16, 15, 18, 17)
SIGNS = (1, -1)


def side(move):
    return 0 if move == 1 else 1


def moves(sign):
    return [tuple(sign * c for c in v) for v in VEL]


def order_along(which, sign):
    place = {}
    for way in SIGNS:
        count = 0
        for q, m in enumerate(moves(sign)):
            if m[which] == way:
                place[q] = count
                count += 1
    return place


def message_list(merge):
    ys = (1,) if merge else SIGNS
    out = []
    for oz in SIGNS:
        out += [((ox, 0, oz), "xz", (side(ox), 3 + side(oz))) for ox in SIGNS]
        out += [((0, oy, oz), "e", (side(oy), side(oz))) for oy in ys]
        out.append(((0, 0, oz), "z", (side(oz),)))
    for ox in SIGNS:
        out += [((ox, oy, 0), "x", (side(ox), 1 + side(oy))) for oy in ys]
    out += [((0, oy, 0), "yy" if merge else "y", (side(oy),)) for oy in ys]
    out += [((ox, 0, 0), "x", (side(ox), 0)) for ox in SIGNS]
    return out


EARLY = ("xz", "e", "z")


def total(items):
    items = list(items)
    while len(items) > 1:
        nxt = [items[i] + items[i + 1] for i in range(0, len(items) - 1, 2)]
        if len(items) % 2:
            nxt.append(items[-1])
        items = nxt
    return items[0]


def first_moments(f):
    density = total(f)
    flow = []
    for d in range(3):
        plus = total([f[q] for q in range(Q) if VEL[q][d] == 1])
        minus = total([f[q] for q in range(Q) if VEL[q][d] == -1])
        flow.append(plus - minus)
    return density, flow


def along(b):
    bx, by, bz = b
    return {
        1: bx, 3: by, 5: bz,
        7: bx + by, 9: bx - by, 11: bx + bz, 13: bx - bz, 15: by + bz, 17: by - bz,
    }


def collided(f, r, v, alpha, wall):
    vv = v[0] * v[0] + v[1] * v[1] + v[2] * v[2]
    base = 1.0 - 1.5 * vv
    out = [None] * Q
    out[0] = jnp.where(wall, f[0], alpha * f[0] + (WEIGHT[0] * r) * base)
    by_weight = {1: WEIGHT[1] * r, 2: WEIGHT[7] * r}
    for q, cv in along(v).items():
        wr = by_weight[1 if q < 7 else 2]
        even = wr * (base + 4.5 * (cv * cv))
        odd = wr * (3.0 * cv)
        out[q] = jnp.where(wall, f[q + 1], alpha * f[q] + (even + odd))
        out[q + 1] = jnp.where(wall, f[q], alpha * f[q + 1] + (even - odd))
    return out


def pulled_back(g, r, u, cells):
    alpha, beta, keep, damp, wall = cells
    v = [keep * x for x in u]
    sums = {q: g[q] + g[q + 1] for q in range(1, Q, 2)}
    diff = {q: g[q] - g[q + 1] for q in range(1, Q, 2)}
    wa, wb = WEIGHT[1], WEIGHT[7]
    axes = total([sums[1], sums[3], sums[5]])
    diag = total([sums[q] for q in (7, 9, 11, 13, 15, 17)])
    g0 = WEIGHT[0] * g[0] + wa * axes + wb * diag
    gx = wa * diff[1] + wb * ((diff[7] + diff[9]) + (diff[11] + diff[13]))
    gy = wa * diff[3] + wb * ((diff[7] - diff[9]) + (diff[15] + diff[17]))
    gz = wa * diff[5] + wb * ((diff[11] - diff[13]) + (diff[15] - diff[17]))
    xy, xz, yz = sums[7] + sums[9], sums[11] + sums[13], sums[15] + sums[17]
    gxx = wa * sums[1] + wb * (xy + xz)
    gyy = wa * sums[3] + wb * (xy + yz)
    gzz = wa * sums[5] + wb * (xz + yz)
    gxy = wb * (sums[7] - sums[9])
    gxz = wb * (sums[11] - sums[13])
    gyz = wb * (sums[15] - sums[17])
    hx = 4.5 * (gxx * v[0] + gxy * v[1] + gxz * v[2]) - 1.5 * g0 * v[0]
    hy = 4.5 * (gxy * v[0] + gyy * v[1] + gyz * v[2]) - 1.5 * g0 * v[1]
    hz = 4.5 * (gxz * v[0] + gyz * v[1] + gzz * v[2]) - 1.5 * g0 * v[2]
    slope = [3.0 * gx + 2.0 * hx, 3.0 * gy + 2.0 * hy, 3.0 * gz + 2.0 * hz]
    quad = v[0] * hx + v[1] * hy + v[2] * hz
    uu = u[0] * u[0] + u[1] * u[1] + u[2] * u[2]
    a0 = beta * (g0 - quad) - damp * uu
    scale = beta * keep
    twice = 2.0 * damp
    b = [scale * s + twice * x for s, x in zip(slope, u)]
    out = [None] * Q
    out[0] = jnp.where(wall, g[0], alpha * g[0] + a0)
    for q, cb in along(b).items():
        out[q] = jnp.where(wall, g[q + 1], alpha * g[q] + (a0 + cb))
        out[q + 1] = jnp.where(wall, g[q], alpha * g[q + 1] + (a0 - cb))
    by_damp = r * (uu - 1.25 * (slope[0] * u[0] + slope[1] * u[1] + slope[2] * u[2]))
    return out, by_damp


class Exchange:
    def __init__(self, signs, nz, refs):
        self.signs = signs
        self.nz = nz
        self.px, self.pq, self.py, self.pe, self.pz = refs[:5]
        self.kept, self.rx, self.ry, self.re, self.rz = refs[5:]
        self.count = 5 * nz
        self.lane = lax.broadcasted_iota(jnp.int32, (8, 128), 1)
        self.row = lax.broadcasted_iota(jnp.int32, (8, 128), 0)
        zero = jnp.zeros((8, 128), jnp.float32)
        self.packed = [zero, zero]
        self.moves = [moves(s) for s in signs]
        self.places = [[order_along(d, s) for d in range(3)] for s in signs]

    def edge_row(self, fi, oy, oz):
        return (fi * 2 + side(oy)) * 2 + side(oz)

    def scatter(self, fi, z, tiles):
        nz = self.nz
        for q in range(Q):
            mx, my, mz = self.moves[fi][q]
            place = self.places[fi]
            t = tiles[q]
            if my:
                t = pltpu.roll(t, my % 8, axis=0)
            flat = t
            if mx:
                t = pltpu.roll(t, mx % 128, axis=1)
            zp = (z + mz) % nz
            wraps = zp != z + mz
            if wraps:
                self.pz[side(mz), fi * 5 + place[2][q]] = t
            else:
                self.kept[fi, q, zp] = t
            if mx:
                k = fi * self.count + place[0][q] * nz + zp
                shift = k + 1 if mx == 1 else k
                moved = pltpu.roll(flat, shift, axis=1) if shift else flat
                s = side(mx)
                self.packed[s] = jnp.where(self.lane == k, moved, self.packed[s])
            if my:
                w = 0 if my == 1 else 7
                s = side(my)
                edge = t[w : w + 1, :]
                if wraps:
                    e = self.edge_row(fi, my, mz)
                    self.pe[e : e + 1, :] = edge
                else:
                    k = fi * self.count + place[1][q] * nz + zp
                    self.py[s, k : k + 1, :] = edge

    def pack(self, target):
        for s in (0, 1):
            target[s] = self.packed[s]

    def gather(self, fi, z, merge, given=None):
        nz = self.nz
        out = []
        for q in range(Q):
            mx, my, mz = self.moves[fi][q]
            place = self.places[fi]
            wraps = (mz == 1 and z == 0) or (mz == -1 and z == nz - 1)
            if wraps:
                t = self.rz[side(mz), fi * 5 + place[2][q]]
            else:
                t = self.kept[fi, q, z]
            sy = 0 if merge else side(my)
            w = 0 if my == 1 else 7
            if my:
                if wraps:
                    e = self.edge_row(fi, my, mz)
                    edge = self.re[sy, side(mz), e : e + 1, :]
                else:
                    k = fi * self.count + place[1][q] * nz + z
                    edge = self.ry[side(my), k : k + 1, :]
                t = jnp.where(self.row == w, jnp.broadcast_to(edge, (8, 128)), t)
            if mx:
                s = side(mx)
                k = fi * self.count + place[0][q] * nz + z
                if wraps:
                    col = self.rx[s, 3 + side(mz)]
                else:
                    col = self.rx[s, 0]
                    if my:
                        col = jnp.where(self.row == w, self.rx[s, 1 + sy], col)
                target = 0 if mx == 1 else 127
                shift = (target - k) % 128
                if shift:
                    col = pltpu.roll(col, shift, axis=1)
                t = jnp.where(self.lane == target, col, t)
            if given is not None and (my or wraps):
                span, depth, tiles = given
                mask = None
                if my:
                    mask = jnp.logical_and(self.row == w, span)
                if wraps:
                    whole = depth[side(mz)]
                    mask = whole if mask is None else jnp.logical_or(mask, whole)
                t = jnp.where(mask, tiles(OPP[q]), t)
            out.append(t)
        return out


def saved_cells(saved, kind, z):
    n = kind[z]
    fluid = n == 0
    alpha = jnp.where(fluid, -0.25, 0.0)
    beta = jnp.where(fluid, 1.25, jnp.where(n == 3, 1.0, 0.0))
    return alpha, beta, saved[z, 4], saved[z, 5], n == 1


def depth_order(nz):
    return [0, nz - 1] + list(range(1, nz - 1))


def window(
    sizes, nz,
    step, pop_hbm, por_hbm, kind_hbm, adj_hbm,
    adj, kind, saved, part, edges, kept2, rx2, ry2, re2, rz2,
    pop, por, load_sem,
    px1, pq1, py1, pe1, pz1, px2, pq2, py2, pe2, pz2,
    kept1, rx1, ry1, re1, rz1,
    send1, recv1, send2, recv2,
):
    merge = sizes[1] == 2
    names = ("gx", "gy", "gz")
    here = [lax.axis_index(n) for n in names]
    messages = message_list(merge)

    pairs = [(por_hbm, por), (kind_hbm, kind)]
    for z in depth_order(nz):
        pairs.append((adj_hbm.at[:, z], adj.at[:, z]))
        pairs.append((pop_hbm.at[:, z], pop.at[:, z]))
    loads = [
        pltpu.make_async_copy(src, dst, load_sem.at[i]) for i, (src, dst) in enumerate(pairs)
    ]
    for c in loads:
        c.start()

    def target(offset):
        return {
            n: lax.rem(here[d] + (offset[d] + sizes[d]), sizes[d])
            for d, n in enumerate(names) if offset[d]
        }

    def bounded(offset):
        return (0 if merge else offset[1], offset[2])

    def inside(steps, way):
        ok = None
        for d, move in zip((1, 2), steps):
            if move:
                place = here[d] + way * move
                test = place < sizes[d] if way * move > 0 else place >= 0
                ok = test if ok is None else jnp.logical_and(ok, test)
        return ok

    def guarded(items, way, act):
        groups = {}
        for item in items:
            groups.setdefault(bounded(item[0]), []).append(item)
        for steps, group in groups.items():
            def every(group=group):
                for item in group:
                    act(item)
            ok = inside(steps, way)
            if ok is None:
                every()
            else:
                pl.when(ok)(every)

    barrier = pltpu.get_barrier_semaphore()
    guarded(messages, 1, lambda m: pl.semaphore_signal(
        barrier, inc=1, device_id=target(m[0]), device_id_type=MESH))
    expected = 0
    for offset, _, _ in messages:
        ok = inside(bounded(offset), -1)
        expected = expected + (1 if ok is None else jnp.where(ok, 1, 0))

    def copies(bufs, send, recv):
        px, pq, py, pe, pz, rx, ry, re, rz = bufs
        made = []
        for i, (offset, what, at) in enumerate(messages):
            if what == "x":
                src, dst = px.at[at[0]], rx.at[at[0], at[1]]
            elif what == "xz":
                src, dst = pq.at[at[0]], rx.at[at[0], at[1]]
            elif what == "e":
                src, dst = pe, re.at[at[0], at[1]]
            elif what == "z":
                src, dst = pz.at[at[0]], rz.at[at[0]]
            elif what == "yy":
                src, dst = py.at[here[1]], ry.at[here[1]]
            else:
                src, dst = py.at[at[0]], ry.at[at[0]]
            made.append((offset, what in EARLY, pltpu.make_async_remote_copy(
                src_ref=src, dst_ref=dst, send_sem=send.at[i], recv_sem=recv.at[i],
                device_id=target(offset), device_id_type=MESH,
            )))
        return made

    def start(made, early):
        guarded([m for m in made if m[1] == early], 1, lambda m: m[2].start())

    def arrive(made):
        guarded(made, -1, lambda m: m[2].wait_recv())

    def leave(made):
        guarded(made, 1, lambda m: m[2].wait_send())

    first = Exchange((1, -1), nz, (px1, pq1, py1, pe1, pz1, kept1, rx1, ry1, re1, rz1))
    second = Exchange((-1,), nz, (px2, pq2, py2, pe2, pz2, kept2, rx2, ry2, re2, rz2))

    pe1[...] = jnp.zeros_like(pe1)
    py1[...] = jnp.zeros_like(py1)
    pe2[...] = jnp.zeros_like(pe2)
    py2[...] = jnp.zeros_like(py2)

    row = first.row
    span = jnp.logical_or(
        jnp.logical_and(row == 0, jnp.full((8, 128), here[1], jnp.int32) == 0),
        jnp.logical_and(row == 7, jnp.full((8, 128), here[1], jnp.int32) == sizes[1] - 1),
    )
    depth = jnp.full((8, 128), here[2], jnp.int32)
    edges[0] = jnp.where(span, 1, 0)
    edges[1] = jnp.where(depth == 0, 1, 0)
    edges[2] = jnp.where(depth == sizes[2] - 1, 1, 0)

    moment = jnp.full((8, 128), jnp.bitwise_and(step[0], 63), jnp.int32)
    angle = moment.astype(jnp.float32) * (2.0 * math.pi / 64.0)
    inlet_speed = 0.1 * (1.0 + 0.8 * jnp.sin(angle))
    zero = jnp.zeros((8, 128), jnp.float32)

    sent1 = copies((px1, pq1, py1, pe1, pz1, rx1, ry1, re1, rz1), send1, recv1)
    sent2 = copies((px2, pq2, py2, pe2, pz2, rx2, ry2, re2, rz2), send2, recv2)
    loads[0].wait()
    loads[1].wait()
    for turn, z in enumerate(depth_order(nz)):
        loads[2 + 2 * turn].wait()
        first.scatter(1, z, [adj[q, z] for q in range(Q)])
        loads[3 + 2 * turn].wait()
        n = kind[z]
        fluid = n == 0
        inlet = n == 2
        wall = n == 1
        denom = 0.1 + por[z]
        k = 0.1 * (1.0 - por[z]) / denom
        alpha = jnp.where(fluid, -0.25, 0.0)
        beta = jnp.where(fluid, 1.25, jnp.where(n == 3, 1.0, 0.0))
        keep = jnp.where(fluid, 1.0 - k, 1.0)
        f = [pop[q, z] for q in range(Q)]
        r, flow = first_moments(f)
        u = [m / r for m in flow]
        v = [
            jnp.where(inlet, inlet_speed, keep * u[0]),
            jnp.where(inlet, zero, keep * u[1]),
            jnp.where(inlet, zero, keep * u[2]),
        ]
        first.scatter(0, z, collided(f, jnp.where(inlet, 1.0, beta * r), v, alpha, wall))
        saved[z, 0] = r
        for d in range(3):
            saved[z, 1 + d] = u[d]
        saved[z, 4] = keep
        saved[z, 5] = jnp.where(fluid, k, 0.0)
        saved[z, 6] = -0.11 / (denom * denom)
        if turn == 1:
            first.pack(pq1)
            pl.semaphore_wait(barrier, expected)
            start(sent1, True)
    first.pack(px1)
    start(sent1, False)
    arrive(sent1)

    for turn, z in enumerate(depth_order(nz)):
        r, flow = first_moments(first.gather(0, z, merge))
        u = [m / r for m in flow]
        a, by_damp = pulled_back(
            first.gather(1, z, merge), r, u, saved_cells(saved, kind, z))
        part[z] = by_damp
        second.scatter(0, z, a)
        if turn == 1:
            second.pack(pq2)
            start(sent2, True)
    second.pack(px2)
    start(sent2, False)
    leave(sent1)
    arrive(sent2)
    leave(sent2)


def last_step(
    merge, nz,
    adj, kind, saved, part, edges, kept, rx, ry, re, rz,
    out_hbm, sens_hbm,
    out, sens, out_sem, sens_sem,
):
    field = Exchange((-1,), nz, (None,) * 5 + (kept, rx, ry, re, rz))
    span = edges[0] == 1
    depth = (edges[1] == 1, edges[2] == 1)
    copies = []
    for z in range(nz):
        g = field.gather(0, z, merge, (span, depth, lambda q, z=z: adj[q, z]))
        u = [saved[z, 1 + d] for d in range(3)]
        a, by_damp = pulled_back(g, saved[z, 0], u, saved_cells(saved, kind, z))
        sens[z] = jnp.where(kind[z] == 0, saved[z, 6] * (part[z] + by_damp), 0.0)
        for q in range(Q):
            out[q, z] = a[q]
        c = pltpu.make_async_copy(out.at[:, z], out_hbm.at[:, z], out_sem.at[z])
        c.start()
        copies.append(c)
    c = pltpu.make_async_copy(sens, sens_hbm, sens_sem)
    c.start()
    copies.append(c)
    for c in copies:
        c.wait()


def packed_shapes(fields, nz):
    rows = -(-fields * 5 * nz // 8) * 8
    return [
        (2, 8, 128), (2, 8, 128), (2, rows, 128), (8, 128), (2, fields * 5, 8, 128),
    ]


def landing_shapes(fields, nz):
    rows = -(-fields * 5 * nz // 8) * 8
    return [
        (fields, Q, nz, 8, 128), (2, 5, 8, 128), (2, rows, 128), (2, 2, 8, 128),
        (2, fields * 5, 8, 128),
    ]


LIMIT = 8 * 1024 * 1024


def on_device(sizes, populations, porosity, node_type, step_index, adjoint_end):
    _, nz, ny, nx = populations.shape
    assert (ny, nx) == (8, 128) and nz >= 2 and 10 * nz <= 128
    f32 = jnp.float32
    i32 = jnp.int32
    merge = sizes[1] == 2
    count = len(message_list(merge))
    any_space = pl.BlockSpec(memory_space=pl.ANY)
    vmem = pl.BlockSpec(memory_space=pltpu.VMEM)
    handed = [
        pltpu.VMEM(populations.shape, f32),
        pltpu.VMEM(node_type.shape, i32),
        pltpu.VMEM((nz, 7, 8, 128), f32),
        pltpu.VMEM(porosity.shape, f32),
        pltpu.VMEM((3, 8, 128), i32),
    ] + [pltpu.VMEM(s, f32) for s in landing_shapes(1, nz)]
    scratch = packed_shapes(2, nz) + packed_shapes(1, nz) + landing_shapes(2, nz)
    state = pl.pallas_call(
        functools.partial(window, sizes, nz),
        out_shape=handed,
        in_specs=[pl.BlockSpec(memory_space=pltpu.SMEM)] + [pl.BlockSpec(memory_space=pltpu.HBM)] * 4,
        out_specs=[vmem] * len(handed),
        scratch_shapes=[
            pltpu.VMEM(populations.shape, f32),
            pltpu.VMEM(porosity.shape, f32),
            pltpu.SemaphoreType.DMA((2 + 2 * nz,)),
        ] + [pltpu.VMEM(s, f32) for s in scratch] + [pltpu.SemaphoreType.DMA((count,))] * 4,
        compiler_params=pltpu.CompilerParams(
            collective_id=0, has_side_effects=True, vmem_limit_bytes=LIMIT),
    )(step_index, *[
        pltpu.with_memory_space_constraint(x, pltpu.HBM)
        for x in (populations, porosity, node_type, adjoint_end)
    ])
    return pl.pallas_call(
        functools.partial(last_step, merge, nz),
        out_shape=(
            jax.ShapeDtypeStruct(populations.shape, f32),
            jax.ShapeDtypeStruct(porosity.shape, f32),
        ),
        in_specs=[vmem] * len(handed),
        out_specs=(any_space, any_space),
        scratch_shapes=[
            pltpu.VMEM(populations.shape, f32),
            pltpu.VMEM(porosity.shape, f32),
            pltpu.SemaphoreType.DMA((nz,)),
            pltpu.SemaphoreType.DMA,
        ],
        compiler_params=pltpu.CompilerParams(vmem_limit_bytes=LIMIT),
    )(*state)


def solution(mesh):
    sizes = tuple(mesh.shape[n] for n in ("gx", "gy", "gz"))
    return jax.shard_map(
        functools.partial(on_device, sizes),
        mesh=mesh,
        in_specs=(
            P(None, "gz", "gy", "gx"),
            P("gz", "gy", "gx"),
            P("gz", "gy", "gx"),
            P(),
            P(None, "gz", "gy", "gx"),
        ),
        out_specs=(P(None, "gz", "gy", "gx"), P("gz", "gy", "gx")),
        check_vma=False,
    )
```

```python
import functools
import math

import jax
import jax.numpy as jnp
from jax import lax
from jax.experimental import pallas as pl
from jax.experimental.pallas import tpu as pltpu
from jax.sharding import PartitionSpec as P

MESH = pl.DeviceIdType.MESH

VEL = (
    (0, 0, 0),
    (1, 0, 0),
    (-1, 0, 0),
    (0, 1, 0),
    (0, -1, 0),
    (0, 0, 1),
    (0, 0, -1),
    (1, 1, 0),
    (-1, -1, 0),
    (1, -1, 0),
    (-1, 1, 0),
    (1, 0, 1),
    (-1, 0, -1),
    (1, 0, -1),
    (-1, 0, 1),
    (0, 1, 1),
    (0, -1, -1),
    (0, 1, -1),
    (0, -1, 1),
)
Q = len(VEL)
WEIGHT = (1.0 / 3.0,) + (1.0 / 18.0,) * 6 + (1.0 / 36.0,) * 12
OPP = (0, 2, 1, 4, 3, 6, 5, 8, 7, 10, 9, 12, 11, 14, 13, 16, 15, 18, 17)
SIGNS = (1, -1)


def side(move):
    return 0 if move == 1 else 1


def moves(sign):
    return [tuple(sign * c for c in v) for v in VEL]


def order_along(which, sign):
    place = {}
    for way in SIGNS:
        count = 0
        for q, m in enumerate(moves(sign)):
            if m[which] == way:
                place[q] = count
                count += 1
    return place


def message_list(merge, fields):
    ys = (1,) if merge else SIGNS
    out = []
    for fi in reversed(range(fields)):
        for oz in SIGNS:
            stage = 0 if fi else 1 + (oz == 1)
            out.append(((0, 0, oz), "z", (side(oz), fi), stage))
        for oy in ys:
            stage = 0 if fi else 3
            out.append(((0, oy, 0), "yy" if merge else "y", (side(oy), fi), stage))
    for oz in SIGNS:
        stage = 1 + (oz == 1)
        out += [((ox, 0, oz), "xz", (side(ox), side(oz)), stage) for ox in SIGNS]
        out += [((0, oy, oz), "e", (side(oy), side(oz)), stage) for oy in ys]
    for ox in SIGNS:
        out += [((ox, oy, 0), "x", (side(ox), 1 + side(oy)), 3) for oy in ys]
    out += [((ox, 0, 0), "x", (side(ox), 0), 3) for ox in SIGNS]
    rank = {"xz": 0, "e": 1, "z": 2, "x": 3, "yy": 4, "y": 4}
    last = {(0, 0): 5}
    return sorted(out, key=lambda m: (
        m[3], last.get(m[0][1:], rank[m[1]]) if m[1] == "x" else rank[m[1]]))


def face_rows(nz):
    return -(-5 * nz // 8) * 8


def total(items):
    items = list(items)
    while len(items) > 1:
        nxt = [items[i] + items[i + 1] for i in range(0, len(items) - 1, 2)]
        if len(items) % 2:
            nxt.append(items[-1])
        items = nxt
    return items[0]


def first_moments(f):
    density = total(f)
    flow = []
    for d in range(3):
        plus = total([f[q] for q in range(Q) if VEL[q][d] == 1])
        minus = total([f[q] for q in range(Q) if VEL[q][d] == -1])
        flow.append(plus - minus)
    return density, flow


def along(b):
    bx, by, bz = b
    return {
        1: bx, 3: by, 5: bz,
        7: bx + by, 9: bx - by, 11: bx + bz, 13: bx - bz, 15: by + bz, 17: by - bz,
    }


def collided(f, r, v, alpha, wall):
    vv = v[0] * v[0] + v[1] * v[1] + v[2] * v[2]
    base = 1.0 - 1.5 * vv
    out = [None] * Q
    out[0] = jnp.where(wall, f[0], alpha * f[0] + (WEIGHT[0] * r) * base)
    by_weight = {1: WEIGHT[1] * r, 2: WEIGHT[7] * r}
    for q, cv in along(v).items():
        wr = by_weight[1 if q < 7 else 2]
        even = wr * (base + 4.5 * (cv * cv))
        odd = wr * (3.0 * cv)
        out[q] = jnp.where(wall, f[q + 1], alpha * f[q] + (even + odd))
        out[q + 1] = jnp.where(wall, f[q], alpha * f[q + 1] + (even - odd))
    return out


def pulled_back(g, r, u, cells):
    alpha, beta, keep, damp, wall = cells
    v = [keep * x for x in u]
    sums = {q: g[q] + g[q + 1] for q in range(1, Q, 2)}
    diff = {q: g[q] - g[q + 1] for q in range(1, Q, 2)}
    wa, wb = WEIGHT[1], WEIGHT[7]
    axes = total([sums[1], sums[3], sums[5]])
    diag = total([sums[q] for q in (7, 9, 11, 13, 15, 17)])
    g0 = WEIGHT[0] * g[0] + wa * axes + wb * diag
    gx = wa * diff[1] + wb * ((diff[7] + diff[9]) + (diff[11] + diff[13]))
    gy = wa * diff[3] + wb * ((diff[7] - diff[9]) + (diff[15] + diff[17]))
    gz = wa * diff[5] + wb * ((diff[11] - diff[13]) + (diff[15] - diff[17]))
    xy, xz, yz = sums[7] + sums[9], sums[11] + sums[13], sums[15] + sums[17]
    gxx = wa * sums[1] + wb * (xy + xz)
    gyy = wa * sums[3] + wb * (xy + yz)
    gzz = wa * sums[5] + wb * (xz + yz)
    gxy = wb * (sums[7] - sums[9])
    gxz = wb * (sums[11] - sums[13])
    gyz = wb * (sums[15] - sums[17])
    hx = 4.5 * (gxx * v[0] + gxy * v[1] + gxz * v[2]) - 1.5 * g0 * v[0]
    hy = 4.5 * (gxy * v[0] + gyy * v[1] + gyz * v[2]) - 1.5 * g0 * v[1]
    hz = 4.5 * (gxz * v[0] + gyz * v[1] + gzz * v[2]) - 1.5 * g0 * v[2]
    slope = [3.0 * gx + 2.0 * hx, 3.0 * gy + 2.0 * hy, 3.0 * gz + 2.0 * hz]
    quad = v[0] * hx + v[1] * hy + v[2] * hz
    uu = u[0] * u[0] + u[1] * u[1] + u[2] * u[2]
    a0 = beta * (g0 - quad) - damp * uu
    scale = beta * keep
    twice = 2.0 * damp
    b = [scale * s + twice * x for s, x in zip(slope, u)]
    out = [None] * Q
    out[0] = jnp.where(wall, g[0], alpha * g[0] + a0)
    for q, cb in along(b).items():
        out[q] = jnp.where(wall, g[q + 1], alpha * g[q] + (a0 + cb))
        out[q + 1] = jnp.where(wall, g[q], alpha * g[q + 1] + (a0 - cb))
    by_damp = r * (uu - 1.25 * (slope[0] * u[0] + slope[1] * u[1] + slope[2] * u[2]))
    return out, by_damp


class Exchange:
    def __init__(self, signs, nz, refs):
        self.signs = signs
        self.nz = nz
        self.px, self.pq, self.py, self.pe, self.pz = refs[:5]
        self.kept, self.rx, self.ry, self.re, self.rz = refs[5:]
        self.count = 5 * nz
        self.rows = face_rows(nz)
        self.lane = lax.broadcasted_iota(jnp.int32, (8, 128), 1)
        self.row = lax.broadcasted_iota(jnp.int32, (8, 128), 0)
        zero = jnp.zeros((8, 128), jnp.float32)
        self.packed = [zero, zero]
        self.moves = [moves(s) for s in signs]
        self.places = [[order_along(d, s) for d in range(3)] for s in signs]

    def edge_row(self, fi, oy):
        return fi * 2 + side(oy)

    def scatter(self, fi, z, tiles):
        nz = self.nz
        for q in range(Q):
            mx, my, mz = self.moves[fi][q]
            place = self.places[fi]
            t = tiles[q]
            if my:
                t = pltpu.roll(t, my % 8, axis=0)
            flat = t
            if mx:
                t = pltpu.roll(t, mx % 128, axis=1)
            zp = (z + mz) % nz
            wraps = zp != z + mz
            if wraps:
                self.pz[side(mz), fi * 5 + place[2][q]] = t
            else:
                self.kept[fi, q, zp] = t
            if mx:
                k = fi * self.count + place[0][q] * nz + zp
                shift = k + 1 if mx == 1 else k
                moved = pltpu.roll(flat, shift, axis=1) if shift else flat
                s = side(mx)
                self.packed[s] = jnp.where(self.lane == k, moved, self.packed[s])
            if my:
                w = 0 if my == 1 else 7
                s = side(my)
                edge = t[w : w + 1, :]
                if wraps:
                    e = self.edge_row(fi, my)
                    self.pe[side(mz), e : e + 1, :] = edge
                else:
                    k = fi * self.rows + place[1][q] * nz + zp
                    self.py[s, k : k + 1, :] = edge

    def pack(self, target, *at):
        for s in (0, 1):
            target[(*at, s)] = self.packed[s]

    def gather(self, fi, z, merge, given=None):
        nz = self.nz
        out = []
        for q in range(Q):
            mx, my, mz = self.moves[fi][q]
            place = self.places[fi]
            wraps = (mz == 1 and z == 0) or (mz == -1 and z == nz - 1)
            if wraps:
                t = self.rz[side(mz), fi * 5 + place[2][q]]
            else:
                t = self.kept[fi, q, z]
            sy = 0 if merge else side(my)
            w = 0 if my == 1 else 7
            if my:
                if wraps:
                    e = self.edge_row(fi, my)
                    edge = self.re[sy, side(mz), e : e + 1, :]
                else:
                    k = fi * self.rows + place[1][q] * nz + z
                    edge = self.ry[side(my), k : k + 1, :]
                t = jnp.where(self.row == w, jnp.broadcast_to(edge, (8, 128)), t)
            if mx:
                s = side(mx)
                k = fi * self.count + place[0][q] * nz + z
                if wraps:
                    col = self.rx[s, 3 + side(mz)]
                else:
                    col = self.rx[s, 0]
                    if my:
                        col = jnp.where(self.row == w, self.rx[s, 1 + sy], col)
                target = 0 if mx == 1 else 127
                shift = (target - k) % 128
                if shift:
                    col = pltpu.roll(col, shift, axis=1)
                t = jnp.where(self.lane == target, col, t)
            if given is not None and (my or wraps):
                span, depth, tiles = given
                mask = None
                if my:
                    mask = jnp.logical_and(self.row == w, span)
                if wraps:
                    whole = depth[side(mz)]
                    mask = whole if mask is None else jnp.logical_or(mask, whole)
                t = jnp.where(mask, tiles(OPP[q]), t)
            out.append(t)
        return out


def saved_cells(saved, kind, z):
    n = kind[z]
    fluid = n == 0
    alpha = jnp.where(fluid, -0.25, 0.0)
    beta = jnp.where(fluid, 1.25, jnp.where(n == 3, 1.0, 0.0))
    return alpha, beta, saved[z, 4], saved[z, 5], n == 1


def depth_order(nz):
    return [0, nz - 1] + list(range(1, nz - 1))


def window(
    sizes, nz,
    step, pop_hbm, por_hbm, kind_hbm, adj_hbm,
    adj, kind, saved, part, edges, kept2, rx2, ry2, re2, rz2,
    pop, por, load_sem,
    px1, pq1, py1, pe1, pz1, px2, pq2, py2, pe2, pz2,
    kept1, rx1, ry1, re1, rz1,
    send1, recv1, send2, recv2,
):
    merge = sizes[1] == 2
    names = ("gx", "gy", "gz")
    here = [lax.axis_index(n) for n in names]
    both, alone = message_list(merge, 2), message_list(merge, 1)

    pairs = [(adj_hbm.at[:, z], adj.at[:, z]) for z in depth_order(nz)]
    pairs += [(por_hbm, por), (kind_hbm, kind)]
    pairs += [(pop_hbm.at[:, z], pop.at[:, z]) for z in depth_order(nz)]
    loads = [
        pltpu.make_async_copy(src, dst, load_sem.at[i]) for i, (src, dst) in enumerate(pairs)
    ]
    for c in loads:
        c.start()

    def target(offset):
        return {
            n: lax.rem(here[d] + (offset[d] + sizes[d]), sizes[d])
            for d, n in enumerate(names) if offset[d]
        }

    def bounded(offset):
        return (0 if merge else offset[1], offset[2])

    def inside(steps, way):
        ok = None
        for d, move in zip((1, 2), steps):
            if move:
                place = here[d] + way * move
                test = place < sizes[d] if way * move > 0 else place >= 0
                ok = test if ok is None else jnp.logical_and(ok, test)
        return ok

    def guarded(items, way, act):
        groups = {}
        for item in items:
            groups.setdefault(bounded(item[0]), []).append(item)
        for steps, group in groups.items():
            def every(group=group):
                for item in group:
                    act(item)
            ok = inside(steps, way)
            if ok is None:
                every()
            else:
                pl.when(ok)(every)

    barrier = pltpu.get_barrier_semaphore()
    guarded(alone, 1, lambda m: pl.semaphore_signal(
        barrier, inc=1, device_id=target(m[0]), device_id_type=MESH))
    expected = 0
    for offset, _, _, _ in alone:
        ok = inside(bounded(offset), -1)
        expected = expected + (1 if ok is None else jnp.where(ok, 1, 0))

    def copies(messages, bufs, send, recv):
        px, pq, py, pe, pz, rx, ry, re, rz = bufs
        made = []
        for i, (offset, what, at, stage) in enumerate(messages):
            if what == "x":
                src, dst = px.at[at[0]], rx.at[at[0], at[1]]
            elif what == "xz":
                src, dst = pq.at[at[1], at[0]], rx.at[at[0], 3 + at[1]]
            elif what == "e":
                src, dst = pe.at[at[1]], re.at[at[0], at[1]]
            elif what == "z":
                part = pl.ds(5 * at[1], 5)
                src, dst = pz.at[at[0], part], rz.at[at[0], part]
            else:
                part = pl.ds(face_rows(nz) * at[1], face_rows(nz))
                way = here[1] if what == "yy" else at[0]
                src, dst = py.at[way, part], ry.at[way, part]
            made.append((offset, stage, pltpu.make_async_remote_copy(
                src_ref=src, dst_ref=dst, send_sem=send.at[i], recv_sem=recv.at[i],
                device_id=target(offset), device_id_type=MESH,
            )))
        return made

    def start(made, stage):
        guarded([m for m in made if m[1] == stage], 1, lambda m: m[2].start())

    def arrive(made):
        guarded(made, -1, lambda m: m[2].wait_recv())

    def leave(made):
        guarded(made, 1, lambda m: m[2].wait_send())

    first = Exchange((1, -1), nz, (px1, pq1, py1, pe1, pz1, kept1, rx1, ry1, re1, rz1))
    second = Exchange((-1,), nz, (px2, pq2, py2, pe2, pz2, kept2, rx2, ry2, re2, rz2))

    pe1[...] = jnp.zeros_like(pe1)
    py1[...] = jnp.zeros_like(py1)
    pe2[...] = jnp.zeros_like(pe2)
    py2[...] = jnp.zeros_like(py2)

    row = first.row
    span = jnp.logical_or(
        jnp.logical_and(row == 0, jnp.full((8, 128), here[1], jnp.int32) == 0),
        jnp.logical_and(row == 7, jnp.full((8, 128), here[1], jnp.int32) == sizes[1] - 1),
    )
    depth = jnp.full((8, 128), here[2], jnp.int32)
    edges[0] = jnp.where(span, 1, 0)
    edges[1] = jnp.where(depth == 0, 1, 0)
    edges[2] = jnp.where(depth == sizes[2] - 1, 1, 0)

    moment = jnp.full((8, 128), jnp.bitwise_and(step[0], 63), jnp.int32)
    angle = moment.astype(jnp.float32) * (2.0 * math.pi / 64.0)
    inlet_speed = 0.1 * (1.0 + 0.8 * jnp.sin(angle))
    zero = jnp.zeros((8, 128), jnp.float32)

    sent1 = copies(both, (px1, pq1, py1, pe1, pz1, rx1, ry1, re1, rz1), send1, recv1)
    sent2 = copies(alone, (px2, pq2, py2, pe2, pz2, rx2, ry2, re2, rz2), send2, recv2)
    for turn, z in enumerate(depth_order(nz)):
        loads[turn].wait()
        first.scatter(1, z, [adj[q, z] for q in range(Q)])
    pl.semaphore_wait(barrier, expected)
    start(sent1, 0)

    loads[nz].wait()
    loads[nz + 1].wait()
    for turn, z in enumerate(depth_order(nz)):
        loads[nz + 2 + turn].wait()
        n = kind[z]
        fluid = n == 0
        inlet = n == 2
        wall = n == 1
        denom = 0.1 + por[z]
        k = 0.1 * (1.0 - por[z]) / denom
        alpha = jnp.where(fluid, -0.25, 0.0)
        beta = jnp.where(fluid, 1.25, jnp.where(n == 3, 1.0, 0.0))
        keep = jnp.where(fluid, 1.0 - k, 1.0)
        f = [pop[q, z] for q in range(Q)]
        r, flow = first_moments(f)
        u = [m / r for m in flow]
        v = [
            jnp.where(inlet, inlet_speed, keep * u[0]),
            jnp.where(inlet, zero, keep * u[1]),
            jnp.where(inlet, zero, keep * u[2]),
        ]
        first.scatter(0, z, collided(f, jnp.where(inlet, 1.0, beta * r), v, alpha, wall))
        saved[z, 0] = r
        for d in range(3):
            saved[z, 1 + d] = u[d]
        saved[z, 4] = keep
        saved[z, 5] = jnp.where(fluid, k, 0.0)
        saved[z, 6] = -0.11 / (denom * denom)
        if turn < 2:
            first.pack(pq1, 1 - turn)
            start(sent1, 1 + turn)
    first.pack(px1)
    start(sent1, 3)
    arrive(sent1)

    for turn, z in enumerate(depth_order(nz)):
        r, flow = first_moments(first.gather(0, z, merge))
        u = [m / r for m in flow]
        a, by_damp = pulled_back(
            first.gather(1, z, merge), r, u, saved_cells(saved, kind, z))
        part[z] = by_damp
        second.scatter(0, z, a)
        if turn < 2:
            second.pack(pq2, 1 - turn)
            start(sent2, 1 + turn)
    second.pack(px2)
    start(sent2, 3)
    leave(sent1)
    arrive(sent2)
    leave(sent2)


def last_step(
    merge, nz,
    adj, kind, saved, part, edges, kept, rx, ry, re, rz,
    out_hbm, sens_hbm,
    out, sens, out_sem, sens_sem,
):
    field = Exchange((-1,), nz, (None,) * 5 + (kept, rx, ry, re, rz))
    span = edges[0] == 1
    depth = (edges[1] == 1, edges[2] == 1)
    copies = []
    for z in range(nz):
        g = field.gather(0, z, merge, (span, depth, lambda q, z=z: adj[q, z]))
        u = [saved[z, 1 + d] for d in range(3)]
        a, by_damp = pulled_back(g, saved[z, 0], u, saved_cells(saved, kind, z))
        sens[z] = jnp.where(kind[z] == 0, saved[z, 6] * (part[z] + by_damp), 0.0)
        for q in range(Q):
            out[q, z] = a[q]
        c = pltpu.make_async_copy(out.at[:, z], out_hbm.at[:, z], out_sem.at[z])
        c.start()
        copies.append(c)
    c = pltpu.make_async_copy(sens, sens_hbm, sens_sem)
    c.start()
    copies.append(c)
    for c in copies:
        c.wait()


def packed_shapes(fields, nz):
    rows = fields * face_rows(nz)
    return [
        (2, 8, 128), (2, 2, 8, 128), (2, rows, 128), (2, 8, 128), (2, fields * 5, 8, 128),
    ]


def landing_shapes(fields, nz):
    rows = fields * face_rows(nz)
    return [
        (fields, Q, nz, 8, 128), (2, 5, 8, 128), (2, rows, 128), (2, 2, 8, 128),
        (2, fields * 5, 8, 128),
    ]


LIMIT = 8 * 1024 * 1024


def on_device(sizes, populations, porosity, node_type, step_index, adjoint_end):
    _, nz, ny, nx = populations.shape
    assert (ny, nx) == (8, 128) and nz >= 2 and 10 * nz <= 128
    f32 = jnp.float32
    i32 = jnp.int32
    merge = sizes[1] == 2
    counts = [len(message_list(merge, fields)) for fields in (2, 2, 1, 1)]
    any_space = pl.BlockSpec(memory_space=pl.ANY)
    vmem = pl.BlockSpec(memory_space=pltpu.VMEM)
    handed = [
        pltpu.VMEM(populations.shape, f32),
        pltpu.VMEM(node_type.shape, i32),
        pltpu.VMEM((nz, 7, 8, 128), f32),
        pltpu.VMEM(porosity.shape, f32),
        pltpu.VMEM((3, 8, 128), i32),
    ] + [pltpu.VMEM(s, f32) for s in landing_shapes(1, nz)]
    scratch = packed_shapes(2, nz) + packed_shapes(1, nz) + landing_shapes(2, nz)
    state = pl.pallas_call(
        functools.partial(window, sizes, nz),
        out_shape=handed,
        in_specs=[pl.BlockSpec(memory_space=pltpu.SMEM)] + [pl.BlockSpec(memory_space=pltpu.HBM)] * 4,
        out_specs=[vmem] * len(handed),
        scratch_shapes=[
            pltpu.VMEM(populations.shape, f32),
            pltpu.VMEM(porosity.shape, f32),
            pltpu.SemaphoreType.DMA((2 + 2 * nz,)),
        ] + [pltpu.VMEM(s, f32) for s in scratch] + [pltpu.SemaphoreType.DMA((c,)) for c in counts],
        compiler_params=pltpu.CompilerParams(
            collective_id=0, has_side_effects=True, vmem_limit_bytes=LIMIT),
    )(step_index, *[
        pltpu.with_memory_space_constraint(x, pltpu.HBM)
        for x in (populations, porosity, node_type, adjoint_end)
    ])
    return pl.pallas_call(
        functools.partial(last_step, merge, nz),
        out_shape=(
            jax.ShapeDtypeStruct(populations.shape, f32),
            jax.ShapeDtypeStruct(porosity.shape, f32),
        ),
        in_specs=[vmem] * len(handed),
        out_specs=(any_space, any_space),
        scratch_shapes=[
            pltpu.VMEM(populations.shape, f32),
            pltpu.VMEM(porosity.shape, f32),
            pltpu.SemaphoreType.DMA((nz,)),
            pltpu.SemaphoreType.DMA,
        ],
        compiler_params=pltpu.CompilerParams(vmem_limit_bytes=LIMIT),
    )(*state)


def solution(mesh):
    sizes = tuple(mesh.shape[n] for n in ("gx", "gy", "gz"))
    return jax.shard_map(
        functools.partial(on_device, sizes),
        mesh=mesh,
        in_specs=(
            P(None, "gz", "gy", "gx"),
            P("gz", "gy", "gx"),
            P("gz", "gy", "gx"),
            P(),
            P(None, "gz", "gy", "gx"),
        ),
        out_specs=(P(None, "gz", "gy", "gx"), P("gz", "gy", "gx")),
        check_vma=False,
    )
```

```python
import functools
import math

import jax
import jax.numpy as jnp
from jax import lax
from jax.experimental import pallas as pl
from jax.experimental.pallas import tpu as pltpu
from jax.sharding import PartitionSpec as P

MESH = pl.DeviceIdType.MESH

VEL = (
    (0, 0, 0),
    (1, 0, 0),
    (-1, 0, 0),
    (0, 1, 0),
    (0, -1, 0),
    (0, 0, 1),
    (0, 0, -1),
    (1, 1, 0),
    (-1, -1, 0),
    (1, -1, 0),
    (-1, 1, 0),
    (1, 0, 1),
    (-1, 0, -1),
    (1, 0, -1),
    (-1, 0, 1),
    (0, 1, 1),
    (0, -1, -1),
    (0, 1, -1),
    (0, -1, 1),
)
Q = len(VEL)
WEIGHT = (1.0 / 3.0,) + (1.0 / 18.0,) * 6 + (1.0 / 36.0,) * 12
OPP = (0, 2, 1, 4, 3, 6, 5, 8, 7, 10, 9, 12, 11, 14, 13, 16, 15, 18, 17)
SIGNS = (1, -1)


def side(move):
    return 0 if move == 1 else 1


def moves(sign):
    return [tuple(sign * c for c in v) for v in VEL]


def order_along(which, sign):
    place = {}
    for way in SIGNS:
        count = 0
        for q, m in enumerate(moves(sign)):
            if m[which] == way:
                place[q] = count
                count += 1
    return place


def face_rows(nz):
    return -(-5 * nz // 8) * 8


def bounded(offset, merge):
    return (0 if merge else offset[1], offset[2])


class Plan:
    def __init__(self, merge, fields, nz):
        ys = (1,) if merge else SIGNS
        found = []
        for oz in SIGNS:
            stage = 1 + (oz == 1)
            found += [((ox, 0, oz), "xz", (side(ox), side(oz)), stage, 1) for ox in SIGNS]
            found += [((0, oy, oz), "e", (side(oy), side(oz)), stage, 1) for oy in ys]
            found.append(((0, 0, oz), "z", (side(oz),), stage, 5 * fields))
        for ox in SIGNS:
            found += [((ox, oy, 0), "xy", (side(ox), side(oy)), 3, 1) for oy in ys]
        for oy in ys:
            found.append(((0, oy, 0), "y", (side(oy),), 3, fields * face_rows(nz) // 8))
        found += [((ox, 0, 0), "x", (side(ox),), 3, 1) for ox in SIGNS]
        self.merge = merge
        self.groups = {}
        for m in found:
            self.groups.setdefault(bounded(m[0], merge), []).append(m)
        self.pieces = {}
        self.place = {}
        self.tiles = 0
        for steps, group in self.groups.items():
            first = self.tiles
            for m in group:
                self.place[m[1], m[2]] = (self.tiles, m[4])
                self.tiles += m[4]
            self.pieces[steps] = (first, self.tiles - first)


def total(items):
    items = list(items)
    while len(items) > 1:
        nxt = [items[i] + items[i + 1] for i in range(0, len(items) - 1, 2)]
        if len(items) % 2:
            nxt.append(items[-1])
        items = nxt
    return items[0]


def first_moments(f):
    density = total(f)
    flow = []
    for d in range(3):
        plus = total([f[q] for q in range(Q) if VEL[q][d] == 1])
        minus = total([f[q] for q in range(Q) if VEL[q][d] == -1])
        flow.append(plus - minus)
    return density, flow


def along(b):
    bx, by, bz = b
    return {
        1: bx, 3: by, 5: bz,
        7: bx + by, 9: bx - by, 11: bx + bz, 13: bx - bz, 15: by + bz, 17: by - bz,
    }


def collided(f, r, v, alpha, wall):
    vv = v[0] * v[0] + v[1] * v[1] + v[2] * v[2]
    base = 1.0 - 1.5 * vv
    out = [None] * Q
    out[0] = jnp.where(wall, f[0], alpha * f[0] + (WEIGHT[0] * r) * base)
    by_weight = {1: WEIGHT[1] * r, 2: WEIGHT[7] * r}
    for q, cv in along(v).items():
        wr = by_weight[1 if q < 7 else 2]
        even = wr * (base + 4.5 * (cv * cv))
        odd = wr * (3.0 * cv)
        out[q] = jnp.where(wall, f[q + 1], alpha * f[q] + (even + odd))
        out[q + 1] = jnp.where(wall, f[q], alpha * f[q + 1] + (even - odd))
    return out


def pulled_back(g, r, u, cells):
    alpha, beta, keep, damp, wall = cells
    v = [keep * x for x in u]
    sums = {q: g[q] + g[q + 1] for q in range(1, Q, 2)}
    diff = {q: g[q] - g[q + 1] for q in range(1, Q, 2)}
    wa, wb = WEIGHT[1], WEIGHT[7]
    axes = total([sums[1], sums[3], sums[5]])
    diag = total([sums[q] for q in (7, 9, 11, 13, 15, 17)])
    g0 = WEIGHT[0] * g[0] + wa * axes + wb * diag
    gx = wa * diff[1] + wb * ((diff[7] + diff[9]) + (diff[11] + diff[13]))
    gy = wa * diff[3] + wb * ((diff[7] - diff[9]) + (diff[15] + diff[17]))
    gz = wa * diff[5] + wb * ((diff[11] - diff[13]) + (diff[15] - diff[17]))
    xy, xz, yz = sums[7] + sums[9], sums[11] + sums[13], sums[15] + sums[17]
    gxx = wa * sums[1] + wb * (xy + xz)
    gyy = wa * sums[3] + wb * (xy + yz)
    gzz = wa * sums[5] + wb * (xz + yz)
    gxy = wb * (sums[7] - sums[9])
    gxz = wb * (sums[11] - sums[13])
    gyz = wb * (sums[15] - sums[17])
    hx = 4.5 * (gxx * v[0] + gxy * v[1] + gxz * v[2]) - 1.5 * g0 * v[0]
    hy = 4.5 * (gxy * v[0] + gyy * v[1] + gyz * v[2]) - 1.5 * g0 * v[1]
    hz = 4.5 * (gxz * v[0] + gyz * v[1] + gzz * v[2]) - 1.5 * g0 * v[2]
    slope = [3.0 * gx + 2.0 * hx, 3.0 * gy + 2.0 * hy, 3.0 * gz + 2.0 * hz]
    quad = v[0] * hx + v[1] * hy + v[2] * hz
    uu = u[0] * u[0] + u[1] * u[1] + u[2] * u[2]
    a0 = beta * (g0 - quad) - damp * uu
    scale = beta * keep
    twice = 2.0 * damp
    b = [scale * s + twice * x for s, x in zip(slope, u)]
    out = [None] * Q
    out[0] = jnp.where(wall, g[0], alpha * g[0] + a0)
    for q, cb in along(b).items():
        out[q] = jnp.where(wall, g[q + 1], alpha * g[q] + (a0 + cb))
        out[q + 1] = jnp.where(wall, g[q], alpha * g[q + 1] + (a0 - cb))
    by_damp = r * (uu - 1.25 * (slope[0] * u[0] + slope[1] * u[1] + slope[2] * u[2]))
    return out, by_damp


class Exchange:
    def __init__(self, signs, nz, plan, refs):
        self.signs = signs
        self.nz = nz
        self.px, self.pq, self.py, self.pe, self.pz = refs[:5]
        self.kept, self.land = refs[5:]
        self.plan = plan
        self.count = 5 * nz
        self.rows = face_rows(nz)
        self.lane = lax.broadcasted_iota(jnp.int32, (8, 128), 1)
        self.row = lax.broadcasted_iota(jnp.int32, (8, 128), 0)
        zero = jnp.zeros((8, 128), jnp.float32)
        self.packed = [zero, zero]
        self.moves = [moves(s) for s in signs]
        self.places = [[order_along(d, s) for d in range(3)] for s in signs]

    def edge_row(self, fi, oy):
        return fi * 2 + side(oy)

    def scatter(self, fi, z, tiles):
        nz = self.nz
        for q in range(Q):
            mx, my, mz = self.moves[fi][q]
            place = self.places[fi]
            t = tiles[q]
            if my:
                t = pltpu.roll(t, my % 8, axis=0)
            flat = t
            if mx:
                t = pltpu.roll(t, mx % 128, axis=1)
            zp = (z + mz) % nz
            wraps = zp != z + mz
            if wraps:
                self.pz[side(mz), fi * 5 + place[2][q]] = t
            else:
                self.kept[fi, q, zp] = t
            if mx:
                k = fi * self.count + place[0][q] * nz + zp
                shift = k + 1 if mx == 1 else k
                moved = pltpu.roll(flat, shift, axis=1) if shift else flat
                s = side(mx)
                self.packed[s] = jnp.where(self.lane == k, moved, self.packed[s])
            if my:
                w = 0 if my == 1 else 7
                s = side(my)
                edge = t[w : w + 1, :]
                if wraps:
                    e = self.edge_row(fi, my)
                    self.pe[side(mz), e : e + 1, :] = edge
                else:
                    k = fi * self.rows + place[1][q] * nz + zp
                    self.py[s, k // 8, k % 8 : k % 8 + 1, :] = edge

    def pack(self, target, *at):
        for s in (0, 1):
            target[(*at, s)] = self.packed[s]

    def landed(self, what, *at):
        if self.plan.merge and what in ("xy", "e", "y"):
            at = {"xy": at[:1] + (0,), "e": (0,) + at[1:], "y": (0,)}[what]
        return self.plan.place[what, at][0]

    def gather(self, fi, z, given=None):
        nz = self.nz
        land = self.land
        out = []
        for q in range(Q):
            mx, my, mz = self.moves[fi][q]
            place = self.places[fi]
            wraps = (mz == 1 and z == 0) or (mz == -1 and z == nz - 1)
            if wraps:
                t = land[self.landed("z", side(mz)) + fi * 5 + place[2][q]]
            else:
                t = self.kept[fi, q, z]
            w = 0 if my == 1 else 7
            if my:
                if wraps:
                    e = self.edge_row(fi, my)
                    edge = land[self.landed("e", side(my), side(mz)), e : e + 1, :]
                else:
                    k = fi * self.rows + place[1][q] * nz + z
                    edge = land[self.landed("y", side(my)) + k // 8, k % 8 : k % 8 + 1, :]
                t = jnp.where(self.row == w, jnp.broadcast_to(edge, (8, 128)), t)
            if mx:
                s = side(mx)
                k = fi * self.count + place[0][q] * nz + z
                if wraps:
                    col = land[self.landed("xz", s, side(mz))]
                else:
                    col = land[self.landed("x", s)]
                    if my:
                        col = jnp.where(self.row == w, land[self.landed("xy", s, side(my))], col)
                target = 0 if mx == 1 else 127
                shift = (target - k) % 128
                if shift:
                    col = pltpu.roll(col, shift, axis=1)
                t = jnp.where(self.lane == target, col, t)
            if given is not None and (my or wraps):
                span, depth, tiles = given
                mask = None
                if my:
                    mask = jnp.logical_and(self.row == w, span)
                if wraps:
                    whole = depth[side(mz)]
                    mask = whole if mask is None else jnp.logical_or(mask, whole)
                t = jnp.where(mask, tiles(OPP[q]), t)
            out.append(t)
        return out


def saved_cells(saved, kind, z):
    n = kind[z]
    fluid = n == 0
    alpha = jnp.where(fluid, -0.25, 0.0)
    beta = jnp.where(fluid, 1.25, jnp.where(n == 3, 1.0, 0.0))
    return alpha, beta, saved[z, 4], saved[z, 5], n == 1


def depth_order(nz):
    return [0, nz - 1] + list(range(1, nz - 1))


def window(
    sizes, nz,
    step, pop_hbm, por_hbm, kind_hbm, adj_hbm,
    adj, kind, saved, part, edges, kept2, land2,
    pop, por, load_sem,
    px1, pq1, py1, pe1, pz1, px2, pq2, py2, pe2, pz2,
    kept1, land1,
    send1, recv1, send2, recv2,
):
    merge = sizes[1] == 2
    names = ("gx", "gy", "gz")
    here = [lax.axis_index(n) for n in names]
    both, alone = Plan(merge, 2, nz), Plan(merge, 1, nz)

    def target(offset):
        return {
            n: lax.rem(here[d] + (offset[d] + sizes[d]), sizes[d])
            for d, n in enumerate(names) if offset[d]
        }

    def inside(steps, way):
        ok = None
        for d, move in zip((1, 2), steps):
            if move:
                place = here[d] + way * move
                test = place < sizes[d] if way * move > 0 else place >= 0
                ok = test if ok is None else jnp.logical_and(ok, test)
        return ok

    def guarded(steps, way, act):
        ok = inside(steps, way)
        if ok is None:
            act()
        else:
            pl.when(ok)(act)

    barrier = pltpu.get_barrier_semaphore()
    expected = 0
    for steps, group in alone.groups.items():
        def greet(group=group):
            for m in group:
                pl.semaphore_signal(
                    barrier, inc=1, device_id=target(m[0]), device_id_type=MESH)
        guarded(steps, 1, greet)
        ok = inside(steps, -1)
        expected = expected + (len(group) if ok is None else jnp.where(ok, len(group), 0))

    pairs = [(pop_hbm, pop), (adj_hbm, adj), (por_hbm, por), (kind_hbm, kind)]
    loads = [
        pltpu.make_async_copy(src, dst, load_sem.at[i]) for i, (src, dst) in enumerate(pairs)
    ]
    for c in loads:
        c.start()

    def source(what, at, bufs):
        px, pq, py, pe, pz = bufs
        if what in ("x", "xy"):
            return px.at[pl.ds(at[0], 1)]
        if what == "xz":
            return pq.at[at[1], pl.ds(at[0], 1)]
        if what == "e":
            return pe.at[pl.ds(at[1], 1)]
        if what == "z":
            return pz.at[at[0]]
        return py.at[here[1] if merge else at[0]]

    def start(plan, bufs, land, sems, stages):
        for i, (steps, group) in enumerate(plan.groups.items()):
            chosen = [m for m in group if m[3] in stages]
            def send(i=i, chosen=chosen):
                for offset, what, at, _, _ in chosen:
                    pltpu.make_async_remote_copy(
                        src_ref=source(what, at, bufs),
                        dst_ref=land.at[pl.ds(*plan.place[what, at])],
                        send_sem=sems[0].at[i], recv_sem=sems[1].at[i],
                        device_id=target(offset), device_id_type=MESH,
                    ).start()
            if chosen:
                guarded(steps, 1, send)

    def settle(plan, land, sem, way):
        for i, (steps, piece) in enumerate(plan.pieces.items()):
            whole = land.at[pl.ds(*piece)]
            guarded(steps, way, pltpu.make_async_copy(whole, whole, sem.at[i]).wait)

    first = Exchange((1, -1), nz, both, (px1, pq1, py1, pe1, pz1, kept1, land1))
    second = Exchange((-1,), nz, alone, (px2, pq2, py2, pe2, pz2, kept2, land2))

    pe1[...] = jnp.zeros_like(pe1)
    py1[...] = jnp.zeros_like(py1)
    pe2[...] = jnp.zeros_like(pe2)
    py2[...] = jnp.zeros_like(py2)

    row = first.row
    span = jnp.logical_or(
        jnp.logical_and(row == 0, jnp.full((8, 128), here[1], jnp.int32) == 0),
        jnp.logical_and(row == 7, jnp.full((8, 128), here[1], jnp.int32) == sizes[1] - 1),
    )
    depth = jnp.full((8, 128), here[2], jnp.int32)
    edges[0] = jnp.where(span, 1, 0)
    edges[1] = jnp.where(depth == 0, 1, 0)
    edges[2] = jnp.where(depth == sizes[2] - 1, 1, 0)

    moment = jnp.full((8, 128), jnp.bitwise_and(step[0], 63), jnp.int32)
    angle = moment.astype(jnp.float32) * (2.0 * math.pi / 64.0)
    inlet_speed = 0.1 * (1.0 + 0.8 * jnp.sin(angle))
    zero = jnp.zeros((8, 128), jnp.float32)

    packs1 = (px1, pq1, py1, pe1, pz1)
    packs2 = (px2, pq2, py2, pe2, pz2)
    for c in loads:
        c.wait()
    for turn, z in enumerate(depth_order(nz)):
        first.scatter(1, z, [adj[q, z] for q in range(Q)])
        n = kind[z]
        fluid = n == 0
        inlet = n == 2
        wall = n == 1
        denom = 0.1 + por[z]
        k = 0.1 * (1.0 - por[z]) / denom
        alpha = jnp.where(fluid, -0.25, 0.0)
        beta = jnp.where(fluid, 1.25, jnp.where(n == 3, 1.0, 0.0))
        keep = jnp.where(fluid, 1.0 - k, 1.0)
        f = [pop[q, z] for q in range(Q)]
        r, flow = first_moments(f)
        u = [m / r for m in flow]
        v = [
            jnp.where(inlet, inlet_speed, keep * u[0]),
            jnp.where(inlet, zero, keep * u[1]),
            jnp.where(inlet, zero, keep * u[2]),
        ]
        first.scatter(0, z, collided(f, jnp.where(inlet, 1.0, beta * r), v, alpha, wall))
        saved[z, 0] = r
        for d in range(3):
            saved[z, 1 + d] = u[d]
        saved[z, 4] = keep
        saved[z, 5] = jnp.where(fluid, k, 0.0)
        saved[z, 6] = -0.11 / (denom * denom)
        if turn < 2:
            first.pack(pq1, 1 - turn)
    first.pack(px1)
    pl.semaphore_wait(barrier, expected)
    start(both, packs1, land1, (send1, recv1), (1, 2, 3))
    settle(both, land1, recv1, -1)

    for turn, z in enumerate(depth_order(nz)):
        r, flow = first_moments(first.gather(0, z))
        u = [m / r for m in flow]
        a, by_damp = pulled_back(
            first.gather(1, z), r, u, saved_cells(saved, kind, z))
        part[z] = by_damp
        second.scatter(0, z, a)
        if turn < 2:
            second.pack(pq2, 1 - turn)
            start(alone, packs2, land2, (send2, recv2), (1 + turn,))
    second.pack(px2)
    start(alone, packs2, land2, (send2, recv2), (3,))
    settle(both, land1, send1, 1)
    settle(alone, land2, recv2, -1)
    settle(alone, land2, send2, 1)


def last_step(
    merge, nz,
    adj, kind, saved, part, edges, kept, land,
    out_hbm, sens_hbm,
    out, sens, out_sem, sens_sem,
):
    field = Exchange((-1,), nz, Plan(merge, 1, nz), (None,) * 5 + (kept, land))
    span = edges[0] == 1
    depth = (edges[1] == 1, edges[2] == 1)
    copies = []
    for z in range(nz):
        g = field.gather(0, z, (span, depth, lambda q, z=z: adj[q, z]))
        u = [saved[z, 1 + d] for d in range(3)]
        a, by_damp = pulled_back(g, saved[z, 0], u, saved_cells(saved, kind, z))
        sens[z] = jnp.where(kind[z] == 0, saved[z, 6] * (part[z] + by_damp), 0.0)
        for q in range(Q):
            out[q, z] = a[q]
        c = pltpu.make_async_copy(out.at[:, z], out_hbm.at[:, z], out_sem.at[z])
        c.start()
        copies.append(c)
    c = pltpu.make_async_copy(sens, sens_hbm, sens_sem)
    c.start()
    copies.append(c)
    for c in copies:
        c.wait()


def packed_shapes(fields, nz):
    return [
        (2, 8, 128), (2, 2, 8, 128), (2, fields * face_rows(nz) // 8, 8, 128),
        (2, 8, 128), (2, fields * 5, 8, 128),
    ]


def landing_shapes(plan, fields, nz):
    return [(fields, Q, nz, 8, 128), (plan.tiles, 8, 128)]


LIMIT = 8 * 1024 * 1024


def on_device(sizes, populations, porosity, node_type, step_index, adjoint_end):
    _, nz, ny, nx = populations.shape
    assert (ny, nx) == (8, 128) and nz >= 2 and 10 * nz <= 128
    f32 = jnp.float32
    i32 = jnp.int32
    merge = sizes[1] == 2
    both, alone = Plan(merge, 2, nz), Plan(merge, 1, nz)
    groups = pltpu.SemaphoreType.DMA((len(both.groups),))
    any_space = pl.BlockSpec(memory_space=pl.ANY)
    vmem = pl.BlockSpec(memory_space=pltpu.VMEM)
    handed = [
        pltpu.VMEM(populations.shape, f32),
        pltpu.VMEM(node_type.shape, i32),
        pltpu.VMEM((nz, 7, 8, 128), f32),
        pltpu.VMEM(porosity.shape, f32),
        pltpu.VMEM((3, 8, 128), i32),
    ] + [pltpu.VMEM(s, f32) for s in landing_shapes(alone, 1, nz)]
    scratch = packed_shapes(2, nz) + packed_shapes(1, nz) + landing_shapes(both, 2, nz)
    state = pl.pallas_call(
        functools.partial(window, sizes, nz),
        out_shape=handed,
        in_specs=[pl.BlockSpec(memory_space=pltpu.SMEM)] + [pl.BlockSpec(memory_space=pltpu.HBM)] * 4,
        out_specs=[vmem] * len(handed),
        scratch_shapes=[
            pltpu.VMEM(populations.shape, f32),
            pltpu.VMEM(porosity.shape, f32),
            pltpu.SemaphoreType.DMA((4,)),
        ] + [pltpu.VMEM(s, f32) for s in scratch] + [groups] * 4,
        compiler_params=pltpu.CompilerParams(
            collective_id=0, has_side_effects=True, vmem_limit_bytes=LIMIT),
    )(step_index, *[
        pltpu.with_memory_space_constraint(x, pltpu.HBM)
        for x in (populations, porosity, node_type, adjoint_end)
    ])
    return pl.pallas_call(
        functools.partial(last_step, merge, nz),
        out_shape=(
            jax.ShapeDtypeStruct(populations.shape, f32),
            jax.ShapeDtypeStruct(porosity.shape, f32),
        ),
        in_specs=[vmem] * len(handed),
        out_specs=(any_space, any_space),
        scratch_shapes=[
            pltpu.VMEM(populations.shape, f32),
            pltpu.VMEM(porosity.shape, f32),
            pltpu.SemaphoreType.DMA((nz,)),
            pltpu.SemaphoreType.DMA,
        ],
        compiler_params=pltpu.CompilerParams(vmem_limit_bytes=LIMIT),
    )(*state)


def solution(mesh):
    sizes = tuple(mesh.shape[n] for n in ("gx", "gy", "gz"))
    return jax.shard_map(
        functools.partial(on_device, sizes),
        mesh=mesh,
        in_specs=(
            P(None, "gz", "gy", "gx"),
            P("gz", "gy", "gx"),
            P("gz", "gy", "gx"),
            P(),
            P(None, "gz", "gy", "gx"),
        ),
        out_specs=(P(None, "gz", "gy", "gx"), P("gz", "gy", "gx")),
        check_vma=False,
    )
```

```python
import functools
import math

import jax
import jax.numpy as jnp
from jax import lax
from jax.experimental import pallas as pl
from jax.experimental.pallas import tpu as pltpu
from jax.sharding import PartitionSpec as P

MESH = pl.DeviceIdType.MESH

VEL = (
    (0, 0, 0),
    (1, 0, 0),
    (-1, 0, 0),
    (0, 1, 0),
    (0, -1, 0),
    (0, 0, 1),
    (0, 0, -1),
    (1, 1, 0),
    (-1, -1, 0),
    (1, -1, 0),
    (-1, 1, 0),
    (1, 0, 1),
    (-1, 0, -1),
    (1, 0, -1),
    (-1, 0, 1),
    (0, 1, 1),
    (0, -1, -1),
    (0, 1, -1),
    (0, -1, 1),
)
Q = len(VEL)
WEIGHT = (1.0 / 3.0,) + (1.0 / 18.0,) * 6 + (1.0 / 36.0,) * 12
OPP = (0, 2, 1, 4, 3, 6, 5, 8, 7, 10, 9, 12, 11, 14, 13, 16, 15, 18, 17)
SIGNS = (1, -1)


def side(move):
    return 0 if move == 1 else 1


def moves(sign):
    return [tuple(sign * c for c in v) for v in VEL]


def order_along(which, sign):
    place = {}
    for way in SIGNS:
        count = 0
        for q, m in enumerate(moves(sign)):
            if m[which] == way:
                place[q] = count
                count += 1
    return place


def face_rows(nz):
    return -(-5 * nz // 8) * 8


def bounded(offset, merge):
    return (0 if merge else offset[1], offset[2])


class Plan:
    def __init__(self, merge, fields, nz):
        ys = (1,) if merge else SIGNS
        found = []
        for oz in SIGNS:
            stage = 1 + (oz == 1)
            found += [((ox, 0, oz), "xz", (side(ox), side(oz)), stage, 1) for ox in SIGNS]
            found += [((0, oy, oz), "e", (side(oy), side(oz)), stage, 1) for oy in ys]
            found.append(((0, 0, oz), "z", (side(oz),), stage, 5 * fields))
        for ox in SIGNS:
            found += [((ox, oy, 0), "xy", (side(ox), side(oy)), 3, 1) for oy in ys]
        for oy in ys:
            found.append(((0, oy, 0), "y", (side(oy),), 3, fields * face_rows(nz) // 8))
        found += [((ox, 0, 0), "x", (side(ox),), 3, 1) for ox in SIGNS]
        self.merge = merge
        self.groups = {}
        for m in found:
            self.groups.setdefault(bounded(m[0], merge), []).append(m)
        self.pieces = {}
        self.place = {}
        self.tiles = 0
        for steps, group in self.groups.items():
            first = self.tiles
            for m in group:
                self.place[m[1], m[2]] = (self.tiles, m[4])
                self.tiles += m[4]
            self.pieces[steps] = (first, self.tiles - first)


def total(items):
    items = list(items)
    while len(items) > 1:
        nxt = [items[i] + items[i + 1] for i in range(0, len(items) - 1, 2)]
        if len(items) % 2:
            nxt.append(items[-1])
        items = nxt
    return items[0]


def first_moments(f):
    density = total(f)
    flow = []
    for d in range(3):
        plus = total([f[q] for q in range(Q) if VEL[q][d] == 1])
        minus = total([f[q] for q in range(Q) if VEL[q][d] == -1])
        flow.append(plus - minus)
    return density, flow


def along(b):
    bx, by, bz = b
    return {
        1: bx, 3: by, 5: bz,
        7: bx + by, 9: bx - by, 11: bx + bz, 13: bx - bz, 15: by + bz, 17: by - bz,
    }


def collided(f, r, v, alpha, wall):
    vv = v[0] * v[0] + v[1] * v[1] + v[2] * v[2]
    base = 1.0 - 1.5 * vv
    out = [None] * Q
    out[0] = jnp.where(wall, f[0], alpha * f[0] + (WEIGHT[0] * r) * base)
    by_weight = {1: WEIGHT[1] * r, 2: WEIGHT[7] * r}
    for q, cv in along(v).items():
        wr = by_weight[1 if q < 7 else 2]
        even = wr * (base + 4.5 * (cv * cv))
        odd = wr * (3.0 * cv)
        out[q] = jnp.where(wall, f[q + 1], alpha * f[q] + (even + odd))
        out[q + 1] = jnp.where(wall, f[q], alpha * f[q + 1] + (even - odd))
    return out


def pulled_back(g, r, u, cells):
    alpha, beta, keep, damp, wall = cells
    v = [keep * x for x in u]
    sums = {q: g[q] + g[q + 1] for q in range(1, Q, 2)}
    diff = {q: g[q] - g[q + 1] for q in range(1, Q, 2)}
    wa, wb = WEIGHT[1], WEIGHT[7]
    axes = total([sums[1], sums[3], sums[5]])
    diag = total([sums[q] for q in (7, 9, 11, 13, 15, 17)])
    g0 = WEIGHT[0] * g[0] + wa * axes + wb * diag
    gx = wa * diff[1] + wb * ((diff[7] + diff[9]) + (diff[11] + diff[13]))
    gy = wa * diff[3] + wb * ((diff[7] - diff[9]) + (diff[15] + diff[17]))
    gz = wa * diff[5] + wb * ((diff[11] - diff[13]) + (diff[15] - diff[17]))
    xy, xz, yz = sums[7] + sums[9], sums[11] + sums[13], sums[15] + sums[17]
    gxx = wa * sums[1] + wb * (xy + xz)
    gyy = wa * sums[3] + wb * (xy + yz)
    gzz = wa * sums[5] + wb * (xz + yz)
    gxy = wb * (sums[7] - sums[9])
    gxz = wb * (sums[11] - sums[13])
    gyz = wb * (sums[15] - sums[17])
    hx = 4.5 * (gxx * v[0] + gxy * v[1] + gxz * v[2]) - 1.5 * g0 * v[0]
    hy = 4.5 * (gxy * v[0] + gyy * v[1] + gyz * v[2]) - 1.5 * g0 * v[1]
    hz = 4.5 * (gxz * v[0] + gyz * v[1] + gzz * v[2]) - 1.5 * g0 * v[2]
    slope = [3.0 * gx + 2.0 * hx, 3.0 * gy + 2.0 * hy, 3.0 * gz + 2.0 * hz]
    quad = v[0] * hx + v[1] * hy + v[2] * hz
    uu = u[0] * u[0] + u[1] * u[1] + u[2] * u[2]
    a0 = beta * (g0 - quad) - damp * uu
    scale = beta * keep
    twice = 2.0 * damp
    b = [scale * s + twice * x for s, x in zip(slope, u)]
    out = [None] * Q
    out[0] = jnp.where(wall, g[0], alpha * g[0] + a0)
    for q, cb in along(b).items():
        out[q] = jnp.where(wall, g[q + 1], alpha * g[q] + (a0 + cb))
        out[q + 1] = jnp.where(wall, g[q], alpha * g[q + 1] + (a0 - cb))
    by_damp = r * (uu - 1.25 * (slope[0] * u[0] + slope[1] * u[1] + slope[2] * u[2]))
    return out, by_damp


class Exchange:
    def __init__(self, signs, nz, plan, refs):
        self.signs = signs
        self.nz = nz
        self.px, self.pq, self.py, self.pe, self.pz = refs[:5]
        self.kept, self.land = refs[5:]
        self.plan = plan
        self.count = 5 * nz
        self.rows = face_rows(nz)
        self.lane = lax.broadcasted_iota(jnp.int32, (8, 128), 1)
        self.row = lax.broadcasted_iota(jnp.int32, (8, 128), 0)
        zero = jnp.zeros((8, 128), jnp.float32)
        self.packed = [zero, zero]
        self.moves = [moves(s) for s in signs]
        self.places = [[order_along(d, s) for d in range(3)] for s in signs]

    def edge_row(self, fi, oy):
        return fi * 2 + side(oy)

    def scatter(self, fi, z, tiles):
        nz = self.nz
        for q in range(Q):
            mx, my, mz = self.moves[fi][q]
            place = self.places[fi]
            t = tiles[q]
            if my:
                t = pltpu.roll(t, my % 8, axis=0)
            flat = t
            if mx:
                t = pltpu.roll(t, mx % 128, axis=1)
            zp = (z + mz) % nz
            wraps = zp != z + mz
            if wraps:
                self.pz[side(mz), fi * 5 + place[2][q]] = t
            else:
                self.kept[fi, q, zp] = t
            if mx:
                k = fi * self.count + place[0][q] * nz + zp
                shift = k + 1 if mx == 1 else k
                moved = pltpu.roll(flat, shift, axis=1) if shift else flat
                s = side(mx)
                self.packed[s] = jnp.where(self.lane == k, moved, self.packed[s])
            if my:
                w = 0 if my == 1 else 7
                s = side(my)
                edge = t[w : w + 1, :]
                if wraps:
                    e = self.edge_row(fi, my)
                    self.pe[side(mz), e : e + 1, :] = edge
                else:
                    k = fi * self.rows + place[1][q] * nz + zp
                    self.py[s, k // 8, k % 8 : k % 8 + 1, :] = edge

    def pack(self, target, *at):
        for s in (0, 1):
            target[(*at, s)] = self.packed[s]

    def landed(self, what, *at):
        if self.plan.merge and what in ("xy", "e", "y"):
            at = {"xy": at[:1] + (0,), "e": (0,) + at[1:], "y": (0,)}[what]
        return self.plan.place[what, at][0]

    def gather(self, fi, z, given=None):
        nz = self.nz
        land = self.land
        out = []
        for q in range(Q):
            mx, my, mz = self.moves[fi][q]
            place = self.places[fi]
            wraps = (mz == 1 and z == 0) or (mz == -1 and z == nz - 1)
            if wraps:
                t = land[self.landed("z", side(mz)) + fi * 5 + place[2][q]]
            else:
                t = self.kept[fi, q, z]
            w = 0 if my == 1 else 7
            if my:
                if wraps:
                    e = self.edge_row(fi, my)
                    edge = land[self.landed("e", side(my), side(mz)), e : e + 1, :]
                else:
                    k = fi * self.rows + place[1][q] * nz + z
                    edge = land[self.landed("y", side(my)) + k // 8, k % 8 : k % 8 + 1, :]
                t = jnp.where(self.row == w, jnp.broadcast_to(edge, (8, 128)), t)
            if mx:
                s = side(mx)
                k = fi * self.count + place[0][q] * nz + z
                if wraps:
                    col = land[self.landed("xz", s, side(mz))]
                else:
                    col = land[self.landed("x", s)]
                    if my:
                        col = jnp.where(self.row == w, land[self.landed("xy", s, side(my))], col)
                target = 0 if mx == 1 else 127
                shift = (target - k) % 128
                if shift:
                    col = pltpu.roll(col, shift, axis=1)
                t = jnp.where(self.lane == target, col, t)
            if given is not None and (my or wraps):
                span, depth, tiles = given
                mask = None
                if my:
                    mask = jnp.logical_and(self.row == w, span)
                if wraps:
                    whole = depth[side(mz)]
                    mask = whole if mask is None else jnp.logical_or(mask, whole)
                t = jnp.where(mask, tiles(OPP[q]), t)
            out.append(t)
        return out


def saved_cells(saved, kind, z):
    n = kind[z]
    fluid = n == 0
    alpha = jnp.where(fluid, -0.25, 0.0)
    beta = jnp.where(fluid, 1.25, jnp.where(n == 3, 1.0, 0.0))
    return alpha, beta, saved[z, 4], saved[z, 5], n == 1


def depth_order(nz):
    return [0, nz - 1] + list(range(1, nz - 1))


def window(
    sizes, nz,
    step, pop_hbm, por_hbm, kind_hbm, adj_hbm,
    adj, kind, saved, part, edges, kept2, land2,
    pop, por, load_sem,
    px1, pq1, py1, pe1, pz1, px2, pq2, py2, pe2, pz2,
    kept1, land1,
    send1, recv1, send2, recv2,
):
    merge = sizes[1] == 2
    names = ("gx", "gy", "gz")
    here = [lax.axis_index(n) for n in names]
    both, alone = Plan(merge, 2, nz), Plan(merge, 1, nz)

    pairs = [(adj_hbm, adj), (pop_hbm, pop), (por_hbm, por), (kind_hbm, kind)]
    loads = [
        pltpu.make_async_copy(src, dst, load_sem.at[i]) for i, (src, dst) in enumerate(pairs)
    ]
    for c in loads:
        c.start()

    def target(offset):
        return {
            n: lax.rem(here[d] + (offset[d] + sizes[d]), sizes[d])
            for d, n in enumerate(names) if offset[d]
        }

    def inside(steps, way):
        ok = None
        for d, move in zip((1, 2), steps):
            if move:
                place = here[d] + way * move
                test = place < sizes[d] if way * move > 0 else place >= 0
                ok = test if ok is None else jnp.logical_and(ok, test)
        return ok

    def guarded(steps, way, act):
        ok = inside(steps, way)
        if ok is None:
            act()
        else:
            pl.when(ok)(act)

    barrier = pltpu.get_barrier_semaphore()
    expected = 0
    for steps, group in alone.groups.items():
        def greet(group=group):
            for m in group:
                pl.semaphore_signal(
                    barrier, inc=1, device_id=target(m[0]), device_id_type=MESH)
        guarded(steps, 1, greet)
        ok = inside(steps, -1)
        expected = expected + (len(group) if ok is None else jnp.where(ok, len(group), 0))

    def source(what, at, bufs):
        px, pq, py, pe, pz = bufs
        if what in ("x", "xy"):
            return px.at[pl.ds(at[0], 1)]
        if what == "xz":
            return pq.at[at[1], pl.ds(at[0], 1)]
        if what == "e":
            return pe.at[pl.ds(at[1], 1)]
        if what == "z":
            return pz.at[at[0]]
        return py.at[here[1] if merge else at[0]]

    def start(plan, bufs, land, sems, stages):
        for i, (steps, group) in enumerate(plan.groups.items()):
            chosen = [m for m in group if m[3] in stages]
            def send(i=i, chosen=chosen):
                for offset, what, at, _, _ in chosen:
                    pltpu.make_async_remote_copy(
                        src_ref=source(what, at, bufs),
                        dst_ref=land.at[pl.ds(*plan.place[what, at])],
                        send_sem=sems[0].at[i], recv_sem=sems[1].at[i],
                        device_id=target(offset), device_id_type=MESH,
                    ).start()
            if chosen:
                guarded(steps, 1, send)

    def settle(plan, land, sem, way):
        for i, (steps, piece) in enumerate(plan.pieces.items()):
            whole = land.at[pl.ds(*piece)]
            guarded(steps, way, pltpu.make_async_copy(whole, whole, sem.at[i]).wait)

    first = Exchange((1, -1), nz, both, (px1, pq1, py1, pe1, pz1, kept1, land1))
    second = Exchange((-1,), nz, alone, (px2, pq2, py2, pe2, pz2, kept2, land2))

    pe1[...] = jnp.zeros_like(pe1)
    py1[...] = jnp.zeros_like(py1)
    pe2[...] = jnp.zeros_like(pe2)
    py2[...] = jnp.zeros_like(py2)

    row = first.row
    span = jnp.logical_or(
        jnp.logical_and(row == 0, jnp.full((8, 128), here[1], jnp.int32) == 0),
        jnp.logical_and(row == 7, jnp.full((8, 128), here[1], jnp.int32) == sizes[1] - 1),
    )
    depth = jnp.full((8, 128), here[2], jnp.int32)
    edges[0] = jnp.where(span, 1, 0)
    edges[1] = jnp.where(depth == 0, 1, 0)
    edges[2] = jnp.where(depth == sizes[2] - 1, 1, 0)

    moment = jnp.full((8, 128), jnp.bitwise_and(step[0], 63), jnp.int32)
    angle = moment.astype(jnp.float32) * (2.0 * math.pi / 64.0)
    inlet_speed = 0.1 * (1.0 + 0.8 * jnp.sin(angle))
    zero = jnp.zeros((8, 128), jnp.float32)

    packs1 = (px1, pq1, py1, pe1, pz1)
    packs2 = (px2, pq2, py2, pe2, pz2)
    loads[0].wait()
    for z in range(nz):
        first.scatter(1, z, [adj[q, z] for q in range(Q)])
    for c in loads[1:]:
        c.wait()
    for turn, z in enumerate(depth_order(nz)):
        n = kind[z]
        fluid = n == 0
        inlet = n == 2
        wall = n == 1
        denom = 0.1 + por[z]
        k = 0.1 * (1.0 - por[z]) / denom
        alpha = jnp.where(fluid, -0.25, 0.0)
        beta = jnp.where(fluid, 1.25, jnp.where(n == 3, 1.0, 0.0))
        keep = jnp.where(fluid, 1.0 - k, 1.0)
        f = [pop[q, z] for q in range(Q)]
        r, flow = first_moments(f)
        u = [m / r for m in flow]
        v = [
            jnp.where(inlet, inlet_speed, keep * u[0]),
            jnp.where(inlet, zero, keep * u[1]),
            jnp.where(inlet, zero, keep * u[2]),
        ]
        first.scatter(0, z, collided(f, jnp.where(inlet, 1.0, beta * r), v, alpha, wall))
        saved[z, 0] = r
        for d in range(3):
            saved[z, 1 + d] = u[d]
        saved[z, 4] = keep
        saved[z, 5] = jnp.where(fluid, k, 0.0)
        saved[z, 6] = -0.11 / (denom * denom)
        if turn < 2:
            first.pack(pq1, 1 - turn)
    first.pack(px1)
    pl.semaphore_wait(barrier, expected)
    start(both, packs1, land1, (send1, recv1), (1, 2, 3))
    settle(both, land1, recv1, -1)

    for turn, z in enumerate(depth_order(nz)):
        r, flow = first_moments(first.gather(0, z))
        u = [m / r for m in flow]
        a, by_damp = pulled_back(
            first.gather(1, z), r, u, saved_cells(saved, kind, z))
        part[z] = by_damp
        second.scatter(0, z, a)
        if turn < 2:
            second.pack(pq2, 1 - turn)
            start(alone, packs2, land2, (send2, recv2), (1 + turn,))
    second.pack(px2)
    start(alone, packs2, land2, (send2, recv2), (3,))
    settle(both, land1, send1, 1)
    settle(alone, land2, recv2, -1)
    settle(alone, land2, send2, 1)


def last_step(
    merge, nz,
    adj, kind, saved, part, edges, kept, land,
    out_hbm, sens_hbm,
    out, sens, out_sem, sens_sem,
):
    field = Exchange((-1,), nz, Plan(merge, 1, nz), (None,) * 5 + (kept, land))
    span = edges[0] == 1
    depth = (edges[1] == 1, edges[2] == 1)
    copies = []
    for z in range(nz):
        g = field.gather(0, z, (span, depth, lambda q, z=z: adj[q, z]))
        u = [saved[z, 1 + d] for d in range(3)]
        a, by_damp = pulled_back(g, saved[z, 0], u, saved_cells(saved, kind, z))
        sens[z] = jnp.where(kind[z] == 0, saved[z, 6] * (part[z] + by_damp), 0.0)
        for q in range(Q):
            out[q, z] = a[q]
        c = pltpu.make_async_copy(out.at[:, z], out_hbm.at[:, z], out_sem.at[z])
        c.start()
        copies.append(c)
    c = pltpu.make_async_copy(sens, sens_hbm, sens_sem)
    c.start()
    copies.append(c)
    for c in copies:
        c.wait()


def packed_shapes(fields, nz):
    return [
        (2, 8, 128), (2, 2, 8, 128), (2, fields * face_rows(nz) // 8, 8, 128),
        (2, 8, 128), (2, fields * 5, 8, 128),
    ]


def landing_shapes(plan, fields, nz):
    return [(fields, Q, nz, 8, 128), (plan.tiles, 8, 128)]


LIMIT = 8 * 1024 * 1024


def on_device(sizes, populations, porosity, node_type, step_index, adjoint_end):
    _, nz, ny, nx = populations.shape
    assert (ny, nx) == (8, 128) and nz >= 2 and 10 * nz <= 128
    f32 = jnp.float32
    i32 = jnp.int32
    merge = sizes[1] == 2
    both, alone = Plan(merge, 2, nz), Plan(merge, 1, nz)
    groups = pltpu.SemaphoreType.DMA((len(both.groups),))
    any_space = pl.BlockSpec(memory_space=pl.ANY)
    vmem = pl.BlockSpec(memory_space=pltpu.VMEM)
    handed = [
        pltpu.VMEM(populations.shape, f32),
        pltpu.VMEM(node_type.shape, i32),
        pltpu.VMEM((nz, 7, 8, 128), f32),
        pltpu.VMEM(porosity.shape, f32),
        pltpu.VMEM((3, 8, 128), i32),
    ] + [pltpu.VMEM(s, f32) for s in landing_shapes(alone, 1, nz)]
    scratch = packed_shapes(2, nz) + packed_shapes(1, nz) + landing_shapes(both, 2, nz)
    state = pl.pallas_call(
        functools.partial(window, sizes, nz),
        out_shape=handed,
        in_specs=[pl.BlockSpec(memory_space=pltpu.SMEM)] + [pl.BlockSpec(memory_space=pltpu.HBM)] * 4,
        out_specs=[vmem] * len(handed),
        scratch_shapes=[
            pltpu.VMEM(populations.shape, f32),
            pltpu.VMEM(porosity.shape, f32),
            pltpu.SemaphoreType.DMA((4,)),
        ] + [pltpu.VMEM(s, f32) for s in scratch] + [groups] * 4,
        compiler_params=pltpu.CompilerParams(
            collective_id=0, has_side_effects=True, vmem_limit_bytes=LIMIT),
    )(step_index, *[
        pltpu.with_memory_space_constraint(x, pltpu.HBM)
        for x in (populations, porosity, node_type, adjoint_end)
    ])
    return pl.pallas_call(
        functools.partial(last_step, merge, nz),
        out_shape=(
            jax.ShapeDtypeStruct(populations.shape, f32),
            jax.ShapeDtypeStruct(porosity.shape, f32),
        ),
        in_specs=[vmem] * len(handed),
        out_specs=(any_space, any_space),
        scratch_shapes=[
            pltpu.VMEM(populations.shape, f32),
            pltpu.VMEM(porosity.shape, f32),
            pltpu.SemaphoreType.DMA((nz,)),
            pltpu.SemaphoreType.DMA,
        ],
        compiler_params=pltpu.CompilerParams(vmem_limit_bytes=LIMIT),
    )(*state)


def solution(mesh):
    sizes = tuple(mesh.shape[n] for n in ("gx", "gy", "gz"))
    return jax.shard_map(
        functools.partial(on_device, sizes),
        mesh=mesh,
        in_specs=(
            P(None, "gz", "gy", "gx"),
            P("gz", "gy", "gx"),
            P("gz", "gy", "gx"),
            P(),
            P(None, "gz", "gy", "gx"),
        ),
        out_specs=(P(None, "gz", "gy", "gx"), P("gz", "gy", "gx")),
        check_vma=False,
    )
```

```python
import functools
import math

import jax
import jax.numpy as jnp
from jax import lax
from jax.experimental import pallas as pl
from jax.experimental.pallas import tpu as pltpu
from jax.sharding import PartitionSpec as P

MESH = pl.DeviceIdType.MESH

VEL = (
    (0, 0, 0),
    (1, 0, 0),
    (-1, 0, 0),
    (0, 1, 0),
    (0, -1, 0),
    (0, 0, 1),
    (0, 0, -1),
    (1, 1, 0),
    (-1, -1, 0),
    (1, -1, 0),
    (-1, 1, 0),
    (1, 0, 1),
    (-1, 0, -1),
    (1, 0, -1),
    (-1, 0, 1),
    (0, 1, 1),
    (0, -1, -1),
    (0, 1, -1),
    (0, -1, 1),
)
Q = len(VEL)
WEIGHT = (1.0 / 3.0,) + (1.0 / 18.0,) * 6 + (1.0 / 36.0,) * 12
OPP = (0, 2, 1, 4, 3, 6, 5, 8, 7, 10, 9, 12, 11, 14, 13, 16, 15, 18, 17)
SIGNS = (1, -1)


def side(move):
    return 0 if move == 1 else 1


def moves(sign):
    return [tuple(sign * c for c in v) for v in VEL]


def order_along(which, sign):
    place = {}
    for way in SIGNS:
        count = 0
        for q, m in enumerate(moves(sign)):
            if m[which] == way:
                place[q] = count
                count += 1
    return place


def face_rows(nz):
    return -(-5 * nz // 8) * 8


def bounded(offset, merge):
    return (0 if merge else offset[1], offset[2])


class Plan:
    def __init__(self, merge, fields, nz):
        ys = (1,) if merge else SIGNS
        found = []
        for oz in SIGNS:
            stage = 1 + (oz == 1)
            found += [((ox, 0, oz), "xz", (side(ox), side(oz)), stage, 1) for ox in SIGNS]
            found += [((0, oy, oz), "e", (side(oy), side(oz)), stage, 1) for oy in ys]
            found.append(((0, 0, oz), "z", (side(oz),), stage, 5 * fields))
        for ox in SIGNS:
            found += [((ox, oy, 0), "xy", (side(ox), side(oy)), 3, 1) for oy in ys]
        for oy in ys:
            found.append(((0, oy, 0), "y", (side(oy),), 3, fields * face_rows(nz) // 8))
        found += [((ox, 0, 0), "x", (side(ox),), 3, 1) for ox in SIGNS]
        self.merge = merge
        self.groups = {}
        for m in found:
            self.groups.setdefault(bounded(m[0], merge), []).append(m)
        self.pieces = {}
        self.place = {}
        self.tiles = 0
        for steps, group in self.groups.items():
            first = self.tiles
            for m in group:
                self.place[m[1], m[2]] = (self.tiles, m[4])
                self.tiles += m[4]
            self.pieces[steps] = (first, self.tiles - first)


def total(items):
    items = list(items)
    while len(items) > 1:
        nxt = [items[i] + items[i + 1] for i in range(0, len(items) - 1, 2)]
        if len(items) % 2:
            nxt.append(items[-1])
        items = nxt
    return items[0]


def first_moments(f):
    density = total(f)
    flow = []
    for d in range(3):
        plus = total([f[q] for q in range(Q) if VEL[q][d] == 1])
        minus = total([f[q] for q in range(Q) if VEL[q][d] == -1])
        flow.append(plus - minus)
    return density, flow


def along(b):
    bx, by, bz = b
    return {
        1: bx, 3: by, 5: bz,
        7: bx + by, 9: bx - by, 11: bx + bz, 13: bx - bz, 15: by + bz, 17: by - bz,
    }


def collided(f, r, v, alpha, wall):
    vv = v[0] * v[0] + v[1] * v[1] + v[2] * v[2]
    base = 1.0 - 1.5 * vv
    out = [None] * Q
    out[0] = jnp.where(wall, f[0], alpha * f[0] + (WEIGHT[0] * r) * base)
    by_weight = {1: WEIGHT[1] * r, 2: WEIGHT[7] * r}
    for q, cv in along(v).items():
        wr = by_weight[1 if q < 7 else 2]
        even = wr * (base + 4.5 * (cv * cv))
        odd = wr * (3.0 * cv)
        out[q] = jnp.where(wall, f[q + 1], alpha * f[q] + (even + odd))
        out[q + 1] = jnp.where(wall, f[q], alpha * f[q + 1] + (even - odd))
    return out


def pulled_back(g, r, u, cells):
    alpha, beta, keep, damp, wall = cells
    v = [keep * x for x in u]
    sums = {q: g[q] + g[q + 1] for q in range(1, Q, 2)}
    diff = {q: g[q] - g[q + 1] for q in range(1, Q, 2)}
    wa, wb = WEIGHT[1], WEIGHT[7]
    axes = total([sums[1], sums[3], sums[5]])
    diag = total([sums[q] for q in (7, 9, 11, 13, 15, 17)])
    g0 = WEIGHT[0] * g[0] + wa * axes + wb * diag
    gx = wa * diff[1] + wb * ((diff[7] + diff[9]) + (diff[11] + diff[13]))
    gy = wa * diff[3] + wb * ((diff[7] - diff[9]) + (diff[15] + diff[17]))
    gz = wa * diff[5] + wb * ((diff[11] - diff[13]) + (diff[15] - diff[17]))
    xy, xz, yz = sums[7] + sums[9], sums[11] + sums[13], sums[15] + sums[17]
    gxx = wa * sums[1] + wb * (xy + xz)
    gyy = wa * sums[3] + wb * (xy + yz)
    gzz = wa * sums[5] + wb * (xz + yz)
    gxy = wb * (sums[7] - sums[9])
    gxz = wb * (sums[11] - sums[13])
    gyz = wb * (sums[15] - sums[17])
    hx = 4.5 * (gxx * v[0] + gxy * v[1] + gxz * v[2]) - 1.5 * g0 * v[0]
    hy = 4.5 * (gxy * v[0] + gyy * v[1] + gyz * v[2]) - 1.5 * g0 * v[1]
    hz = 4.5 * (gxz * v[0] + gyz * v[1] + gzz * v[2]) - 1.5 * g0 * v[2]
    slope = [3.0 * gx + 2.0 * hx, 3.0 * gy + 2.0 * hy, 3.0 * gz + 2.0 * hz]
    quad = v[0] * hx + v[1] * hy + v[2] * hz
    uu = u[0] * u[0] + u[1] * u[1] + u[2] * u[2]
    a0 = beta * (g0 - quad) - damp * uu
    scale = beta * keep
    twice = 2.0 * damp
    b = [scale * s + twice * x for s, x in zip(slope, u)]
    out = [None] * Q
    out[0] = jnp.where(wall, g[0], alpha * g[0] + a0)
    for q, cb in along(b).items():
        out[q] = jnp.where(wall, g[q + 1], alpha * g[q] + (a0 + cb))
        out[q + 1] = jnp.where(wall, g[q], alpha * g[q + 1] + (a0 - cb))
    by_damp = r * (uu - 1.25 * (slope[0] * u[0] + slope[1] * u[1] + slope[2] * u[2]))
    return out, by_damp


class Exchange:
    def __init__(self, signs, nz, plan, refs):
        self.signs = signs
        self.nz = nz
        self.px, self.pq, self.py, self.pe, self.pz = refs[:5]
        self.kept, self.land = refs[5:]
        self.plan = plan
        self.count = 5 * nz
        self.rows = face_rows(nz)
        self.lane = lax.broadcasted_iota(jnp.int32, (8, 128), 1)
        self.row = lax.broadcasted_iota(jnp.int32, (8, 128), 0)
        zero = jnp.zeros((8, 128), jnp.float32)
        self.packed = [zero, zero]
        self.moves = [moves(s) for s in signs]
        self.places = [[order_along(d, s) for d in range(3)] for s in signs]

    def edge_row(self, fi, oy):
        return fi * 2 + side(oy)

    def scatter(self, fi, z, tiles):
        nz = self.nz
        for q in range(Q):
            mx, my, mz = self.moves[fi][q]
            place = self.places[fi]
            t = tiles[q]
            if my:
                t = pltpu.roll(t, my % 8, axis=0)
            flat = t
            if mx:
                t = pltpu.roll(t, mx % 128, axis=1)
            zp = (z + mz) % nz
            wraps = zp != z + mz
            if wraps:
                self.pz[side(mz), fi * 5 + place[2][q]] = t
            else:
                self.kept[fi, q, zp] = t
            if mx:
                k = fi * self.count + place[0][q] * nz + zp
                shift = k + 1 if mx == 1 else k
                moved = pltpu.roll(flat, shift, axis=1) if shift else flat
                s = side(mx)
                self.packed[s] = jnp.where(self.lane == k, moved, self.packed[s])
            if my:
                w = 0 if my == 1 else 7
                s = side(my)
                edge = t[w : w + 1, :]
                if wraps:
                    e = self.edge_row(fi, my)
                    self.pe[side(mz), e : e + 1, :] = edge
                else:
                    k = fi * self.rows + place[1][q] * nz + zp
                    self.py[s, k // 8, k % 8 : k % 8 + 1, :] = edge

    def pack(self, target, *at):
        for s in (0, 1):
            target[(*at, s)] = self.packed[s]

    def landed(self, what, *at):
        if self.plan.merge and what in ("xy", "e", "y"):
            at = {"xy": at[:1] + (0,), "e": (0,) + at[1:], "y": (0,)}[what]
        return self.plan.place[what, at][0]

    def gather(self, fi, z, given=None):
        nz = self.nz
        land = self.land
        out = []
        for q in range(Q):
            mx, my, mz = self.moves[fi][q]
            place = self.places[fi]
            wraps = (mz == 1 and z == 0) or (mz == -1 and z == nz - 1)
            if wraps:
                t = land[self.landed("z", side(mz)) + fi * 5 + place[2][q]]
            else:
                t = self.kept[fi, q, z]
            w = 0 if my == 1 else 7
            if my:
                if wraps:
                    e = self.edge_row(fi, my)
                    edge = land[self.landed("e", side(my), side(mz)), e : e + 1, :]
                else:
                    k = fi * self.rows + place[1][q] * nz + z
                    edge = land[self.landed("y", side(my)) + k // 8, k % 8 : k % 8 + 1, :]
                t = jnp.where(self.row == w, jnp.broadcast_to(edge, (8, 128)), t)
            if mx:
                s = side(mx)
                k = fi * self.count + place[0][q] * nz + z
                if wraps:
                    col = land[self.landed("xz", s, side(mz))]
                else:
                    col = land[self.landed("x", s)]
                    if my:
                        col = jnp.where(self.row == w, land[self.landed("xy", s, side(my))], col)
                target = 0 if mx == 1 else 127
                shift = (target - k) % 128
                if shift:
                    col = pltpu.roll(col, shift, axis=1)
                t = jnp.where(self.lane == target, col, t)
            if given is not None and (my or wraps):
                span, depth, tiles = given
                mask = None
                if my:
                    mask = jnp.logical_and(self.row == w, span)
                if wraps:
                    whole = depth[side(mz)]
                    mask = whole if mask is None else jnp.logical_or(mask, whole)
                t = jnp.where(mask, tiles(OPP[q]), t)
            out.append(t)
        return out


def saved_cells(saved, kind, z):
    n = kind[z]
    fluid = n == 0
    alpha = jnp.where(fluid, -0.25, 0.0)
    beta = jnp.where(fluid, 1.25, jnp.where(n == 3, 1.0, 0.0))
    return alpha, beta, saved[z, 4], saved[z, 5], n == 1


def depth_order(nz):
    return [0, nz - 1] + list(range(1, nz - 1))


def window(
    sizes, nz,
    step, pop_hbm, por_hbm, kind_hbm, adj_hbm,
    adj, kind, saved, part, edges, kept2, land2,
    pop, por, load_sem,
    px1, pq1, py1, pe1, pz1, px2, pq2, py2, pe2, pz2,
    kept1, land1,
    send1, recv1, send2, recv2,
):
    merge = sizes[1] == 2
    names = ("gx", "gy", "gz")
    here = [lax.axis_index(n) for n in names]
    both, alone = Plan(merge, 2, nz), Plan(merge, 1, nz)

    def target(offset):
        return {
            n: lax.rem(here[d] + (offset[d] + sizes[d]), sizes[d])
            for d, n in enumerate(names) if offset[d]
        }

    def inside(steps, way):
        ok = None
        for d, move in zip((1, 2), steps):
            if move:
                place = here[d] + way * move
                test = place < sizes[d] if way * move > 0 else place >= 0
                ok = test if ok is None else jnp.logical_and(ok, test)
        return ok

    def guarded(steps, way, act):
        ok = inside(steps, way)
        if ok is None:
            act()
        else:
            pl.when(ok)(act)

    barrier = pltpu.get_barrier_semaphore()
    expected = 0
    for steps, group in alone.groups.items():
        def greet(group=group):
            for m in group:
                pl.semaphore_signal(
                    barrier, inc=1, device_id=target(m[0]), device_id_type=MESH)
        guarded(steps, 1, greet)
        ok = inside(steps, -1)
        expected = expected + (len(group) if ok is None else jnp.where(ok, len(group), 0))

    pairs = [(pop_hbm, pop), (adj_hbm, adj), (por_hbm, por), (kind_hbm, kind)]
    loads = [
        pltpu.make_async_copy(src, dst, load_sem.at[i]) for i, (src, dst) in enumerate(pairs)
    ]
    for c in loads:
        c.start()

    def source(what, at, bufs):
        px, pq, py, pe, pz = bufs
        if what in ("x", "xy"):
            return px.at[pl.ds(at[0], 1)]
        if what == "xz":
            return pq.at[at[1], pl.ds(at[0], 1)]
        if what == "e":
            return pe.at[pl.ds(at[1], 1)]
        if what == "z":
            return pz.at[at[0]]
        return py.at[here[1] if merge else at[0]]

    def start(plan, bufs, land, sems, stages, skip=()):
        for i, (steps, group) in enumerate(plan.groups.items()):
            chosen = [m for m in group if m[3] in stages and m[1] not in skip]
            def send(i=i, chosen=chosen):
                for offset, what, at, _, _ in chosen:
                    pltpu.make_async_remote_copy(
                        src_ref=source(what, at, bufs),
                        dst_ref=land.at[pl.ds(*plan.place[what, at])],
                        send_sem=sems[0].at[i], recv_sem=sems[1].at[i],
                        device_id=target(offset), device_id_type=MESH,
                    ).start()
            if chosen:
                guarded(steps, 1, send)

    def settle(plan, land, sem, way):
        for i, (steps, piece) in enumerate(plan.pieces.items()):
            whole = land.at[pl.ds(*piece)]
            guarded(steps, way, pltpu.make_async_copy(whole, whole, sem.at[i]).wait)

    first = Exchange((1, -1), nz, both, (px1, pq1, py1, pe1, pz1, kept1, land1))
    second = Exchange((-1,), nz, alone, (px2, pq2, py2, pe2, pz2, kept2, land2))

    pe1[...] = jnp.zeros_like(pe1)
    py1[...] = jnp.zeros_like(py1)
    pe2[...] = jnp.zeros_like(pe2)
    py2[...] = jnp.zeros_like(py2)

    row = first.row
    span = jnp.logical_or(
        jnp.logical_and(row == 0, jnp.full((8, 128), here[1], jnp.int32) == 0),
        jnp.logical_and(row == 7, jnp.full((8, 128), here[1], jnp.int32) == sizes[1] - 1),
    )
    depth = jnp.full((8, 128), here[2], jnp.int32)
    edges[0] = jnp.where(span, 1, 0)
    edges[1] = jnp.where(depth == 0, 1, 0)
    edges[2] = jnp.where(depth == sizes[2] - 1, 1, 0)

    moment = jnp.full((8, 128), jnp.bitwise_and(step[0], 63), jnp.int32)
    angle = moment.astype(jnp.float32) * (2.0 * math.pi / 64.0)
    inlet_speed = 0.1 * (1.0 + 0.8 * jnp.sin(angle))
    zero = jnp.zeros((8, 128), jnp.float32)

    packs1 = (px1, pq1, py1, pe1, pz1)
    packs2 = (px2, pq2, py2, pe2, pz2)
    for c in loads:
        c.wait()
    for turn, z in enumerate(depth_order(nz)):
        first.scatter(1, z, [adj[q, z] for q in range(Q)])
        n = kind[z]
        fluid = n == 0
        inlet = n == 2
        wall = n == 1
        denom = 0.1 + por[z]
        k = 0.1 * (1.0 - por[z]) / denom
        alpha = jnp.where(fluid, -0.25, 0.0)
        beta = jnp.where(fluid, 1.25, jnp.where(n == 3, 1.0, 0.0))
        keep = jnp.where(fluid, 1.0 - k, 1.0)
        f = [pop[q, z] for q in range(Q)]
        r, flow = first_moments(f)
        u = [m / r for m in flow]
        v = [
            jnp.where(inlet, inlet_speed, keep * u[0]),
            jnp.where(inlet, zero, keep * u[1]),
            jnp.where(inlet, zero, keep * u[2]),
        ]
        first.scatter(0, z, collided(f, jnp.where(inlet, 1.0, beta * r), v, alpha, wall))
        saved[z, 0] = r
        for d in range(3):
            saved[z, 1 + d] = u[d]
        saved[z, 4] = keep
        saved[z, 5] = jnp.where(fluid, k, 0.0)
        saved[z, 6] = -0.11 / (denom * denom)
        if turn < 2:
            first.pack(pq1, 1 - turn)
    first.pack(px1)
    pl.semaphore_wait(barrier, expected)
    start(both, packs1, land1, (send1, recv1), (3,), ("x", "y"))
    start(both, packs1, land1, (send1, recv1), (1, 2))
    start(both, packs1, land1, (send1, recv1), (3,), ("xy",))
    settle(both, land1, recv1, -1)

    for turn, z in enumerate(depth_order(nz)):
        r, flow = first_moments(first.gather(0, z))
        u = [m / r for m in flow]
        a, by_damp = pulled_back(
            first.gather(1, z), r, u, saved_cells(saved, kind, z))
        part[z] = by_damp
        second.scatter(0, z, a)
        if turn < 2:
            second.pack(pq2, 1 - turn)
            start(alone, packs2, land2, (send2, recv2), (1 + turn,))
    second.pack(px2)
    start(alone, packs2, land2, (send2, recv2), (3,))
    settle(both, land1, send1, 1)
    settle(alone, land2, recv2, -1)
    settle(alone, land2, send2, 1)


def last_step(
    merge, nz,
    adj, kind, saved, part, edges, kept, land,
    out_hbm, sens_hbm,
    out, sens, out_sem, sens_sem,
):
    field = Exchange((-1,), nz, Plan(merge, 1, nz), (None,) * 5 + (kept, land))
    span = edges[0] == 1
    depth = (edges[1] == 1, edges[2] == 1)
    copies = []
    for z in range(nz):
        g = field.gather(0, z, (span, depth, lambda q, z=z: adj[q, z]))
        u = [saved[z, 1 + d] for d in range(3)]
        a, by_damp = pulled_back(g, saved[z, 0], u, saved_cells(saved, kind, z))
        sens[z] = jnp.where(kind[z] == 0, saved[z, 6] * (part[z] + by_damp), 0.0)
        for q in range(Q):
            out[q, z] = a[q]
        c = pltpu.make_async_copy(out.at[:, z], out_hbm.at[:, z], out_sem.at[z])
        c.start()
        copies.append(c)
    c = pltpu.make_async_copy(sens, sens_hbm, sens_sem)
    c.start()
    copies.append(c)
    for c in copies:
        c.wait()


def packed_shapes(fields, nz):
    return [
        (2, 8, 128), (2, 2, 8, 128), (2, fields * face_rows(nz) // 8, 8, 128),
        (2, 8, 128), (2, fields * 5, 8, 128),
    ]


def landing_shapes(plan, fields, nz):
    return [(fields, Q, nz, 8, 128), (plan.tiles, 8, 128)]


LIMIT = 8 * 1024 * 1024


def on_device(sizes, populations, porosity, node_type, step_index, adjoint_end):
    _, nz, ny, nx = populations.shape
    assert (ny, nx) == (8, 128) and nz >= 2 and 10 * nz <= 128
    f32 = jnp.float32
    i32 = jnp.int32
    merge = sizes[1] == 2
    both, alone = Plan(merge, 2, nz), Plan(merge, 1, nz)
    groups = pltpu.SemaphoreType.DMA((len(both.groups),))
    any_space = pl.BlockSpec(memory_space=pl.ANY)
    vmem = pl.BlockSpec(memory_space=pltpu.VMEM)
    handed = [
        pltpu.VMEM(populations.shape, f32),
        pltpu.VMEM(node_type.shape, i32),
        pltpu.VMEM((nz, 7, 8, 128), f32),
        pltpu.VMEM(porosity.shape, f32),
        pltpu.VMEM((3, 8, 128), i32),
    ] + [pltpu.VMEM(s, f32) for s in landing_shapes(alone, 1, nz)]
    scratch = packed_shapes(2, nz) + packed_shapes(1, nz) + landing_shapes(both, 2, nz)
    state = pl.pallas_call(
        functools.partial(window, sizes, nz),
        out_shape=handed,
        in_specs=[pl.BlockSpec(memory_space=pltpu.SMEM)] + [pl.BlockSpec(memory_space=pltpu.HBM)] * 4,
        out_specs=[vmem] * len(handed),
        scratch_shapes=[
            pltpu.VMEM(populations.shape, f32),
            pltpu.VMEM(porosity.shape, f32),
            pltpu.SemaphoreType.DMA((4,)),
        ] + [pltpu.VMEM(s, f32) for s in scratch] + [groups] * 4,
        compiler_params=pltpu.CompilerParams(
            collective_id=0, has_side_effects=True, vmem_limit_bytes=LIMIT),
    )(step_index, *[
        pltpu.with_memory_space_constraint(x, pltpu.HBM)
        for x in (populations, porosity, node_type, adjoint_end)
    ])
    return pl.pallas_call(
        functools.partial(last_step, merge, nz),
        out_shape=(
            jax.ShapeDtypeStruct(populations.shape, f32),
            jax.ShapeDtypeStruct(porosity.shape, f32),
        ),
        in_specs=[vmem] * len(handed),
        out_specs=(any_space, any_space),
        scratch_shapes=[
            pltpu.VMEM(populations.shape, f32),
            pltpu.VMEM(porosity.shape, f32),
            pltpu.SemaphoreType.DMA((nz,)),
            pltpu.SemaphoreType.DMA,
        ],
        compiler_params=pltpu.CompilerParams(vmem_limit_bytes=LIMIT),
    )(*state)


def solution(mesh):
    sizes = tuple(mesh.shape[n] for n in ("gx", "gy", "gz"))
    return jax.shard_map(
        functools.partial(on_device, sizes),
        mesh=mesh,
        in_specs=(
            P(None, "gz", "gy", "gx"),
            P("gz", "gy", "gx"),
            P("gz", "gy", "gx"),
            P(),
            P(None, "gz", "gy", "gx"),
        ),
        out_specs=(P(None, "gz", "gy", "gx"), P("gz", "gy", "gx")),
        check_vma=False,
    )
```
